128 devices in a mesh: dp: 32 (over y, x, core), tensor: 4 (over z).
Axes of the slice: x: 4, y: 4, z: 4, core: 2. Of those that a mesh axis runs over, the one named last changes fastest.
Arguments:
- attn_heads: bfloat16 [1024, 3584], P('dp', 'tensor'), may hold values from -6 to 6
- out_weight: bfloat16 [3584, 3584], P('tensor'), may hold values from -0.09375 to 0.09375
- residual: bfloat16 [1024, 3584], P(('dp', 'tensor')), may hold values from -6 to 6
- norm_gain: bfloat16 [3584], replicated, may hold values from 0.099609375 to 1.8984375
- shared_gate: bfloat16 [3584], replicated, may hold values from -0.09375 to 0.09375
- shared_gate_proj: bfloat16 [3584, 20480], P(None, ('dp', 'tensor')), may hold values from -0.09375 to 0.09375
- shared_up_proj: bfloat16 [3584, 20480], P(None, ('dp', 'tensor')), may hold values from -0.09375 to 0.09375
- shared_down_proj: bfloat16 [20480, 3584], P(('dp', 'tensor')), may hold values from -0.0390625 to 0.0390625
- expert_gate: bfloat16 [128, 3584, 640], P(('dp', 'tensor')), may hold values from -0.09375 to 0.09375
- expert_up_weight: bfloat16 [128, 3584, 640], P(('dp', 'tensor')), may hold values from -0.09375 to 0.09375
- expert_down: bfloat16 [128, 640, 3584], P(('dp', 'tensor')), may hold values from -0.15625 to 0.15625
- expert_choice: int32 [1024, 8], P(('dp', 'tensor')), may hold values from 0 to 63, all different within a row; in each aligned block of 8 rows (0 to 7, 8 to 15, ...) at most 2 rows name the same one
- gate_probs: float32 [1024, 8], P(('dp', 'tensor')), may hold values from 0.02 to 0.4
Outputs:
- mid: bfloat16 [1024, 3584], P(('dp', 'tensor'))
- ffn_out: bfloat16 [1024, 3584], P(('dp', 'tensor'))
The draws below stay inside these ranges and needn't reach their ends.
Inputs may be any that keep to these rules, and one draw needn't show every extreme that they name: `expert_choice`: the 8 experts of a token differ. Among the 8 rows of one device (aligned blocks) no expert is named more than 2 times, and in every draw some expert is named exactly 2 times in some block.
All inputs are finite; a program needn't handle non-finite values.
Results may differ from the reference program's by a relative error of at most 0.014.
Values may be sent and summed in bfloat16 or wider, within the bound.
A program may use at most 128 MiB of HBM per device.

```python
import math
import jax
import jax.numpy as jnp
import numpy as np
from jax import lax

D = 3584
FF_SH = 20480
FF_E = 1280
TOP = 8
TOK_DEV = 8
HD_ALL = 3584
HALF = 640
EXPERTS = 64
CAP = 2
TOKENS = 1024
DEVICES = 128


def levels(own_key, extent, split, smallest, high):
    loudness, own = 1.0, jax.random.fold_in(own_key, 6)
    for dim, shards_of in split:
        heights = jnp.exp(jax.random.uniform(jax.random.fold_in(own, dim), (shards_of,), jnp.float32, smallest / len(split), high / len(split)))
        loudness = loudness * jnp.repeat(heights, extent[dim] // shards_of).reshape([-1 if axis == dim else 1 for axis in range(len(extent))])
    return loudness


def routed_block(stream_key, own, number, rows, count, top, most, skew):
    order = jax.random.permutation(stream_key, count)
    crowded, ordinary = shares(count, rows * top, most, skew, True), shares(count, rows * top, most, skew, False)
    places = jnp.arange(count)

    def named(tallies, offset_by):
        used = int((tallies > 0).sum())
        fixed = max(1, used // 4)
        moved = fixed + (places - fixed + offset_by * (used - fixed)) % max(1, count - fixed)
        return jnp.zeros((count,), jnp.int32).at[order[jnp.where(places < fixed, places, moved)]].set(jnp.asarray(tallies, jnp.int32))

    tallies = jnp.where(number % 4 == 0, named(crowded, number // 4), named(ordinary, number - number // 4 - 1))
    mixed = jax.random.permutation(jax.random.fold_in(own, 3), count)
    source_of, receiver = mixed[0:count // 2 * 2:2], mixed[1:count // 2 * 2:2]
    slack = jnp.minimum(tallies[source_of] - 1, most - tallies[receiver]) // 2
    slack = jnp.where((source_of == order[0]) | (receiver == order[0]) | (tallies[receiver] == 0), 0, jnp.maximum(slack, 0))
    moved = jax.random.randint(jax.random.fold_in(own, 4), (count // 2,), 0, 1 << 20) % (slack + 1)
    tallies = tallies.at[source_of].add(-moved).at[receiver].add(moved)
    members = jnp.searchsorted(jnp.cumsum(tallies), jnp.arange(rows * top), side="right").astype(jnp.int32)
    table = members.reshape(top, rows).T
    table = table[jax.random.permutation(jax.random.fold_in(own, 1), rows)]
    offset_by = jax.random.randint(jax.random.fold_in(own, 2), (rows, 1), 0, top)
    return jnp.take_along_axis(table, (jnp.arange(top)[None, :] + offset_by) % top, axis=1)


def shares(number_of, total, bound, lean, full):
    portions = [(1 << 20) // math.isqrt(standing ** lean) + 1 for standing in range(1, number_of + 1)]
    largest = bound if full else min(bound, max(-(-total // number_of), total * portions[0] // sum(portions)))
    least = 1 if total - largest >= number_of - 1 else 0
    counts, rest = [largest] + [least] * (number_of - 1), total - largest - least * (number_of - 1)
    while rest > 0:
        free = [i for i in range(1, number_of) if counts[i] < largest] or [i for i in range(1, number_of) if counts[i] < bound]
        pool, left = sum([portions[i] for i in free]), rest
        for i in free:
            addition = min(bound - counts[i], max(1, left * portions[i] // pool), rest)
            counts[i] = counts[i] + addition
            rest = rest - addition
    return np.array(counts)


def normal_values(stream_key, shape, deviation, limit, cuts=(), kind=jnp.bfloat16):
    array = jax.random.normal(stream_key, shape, jnp.float32) * deviation
    if len(cuts) > 0:
        array = levels(stream_key, shape, cuts, -0.22, 0.18) * array
    return jnp.clip(array, min=-limit, max=limit).astype(kind)


def setup_inputs(seed: int = 0) -> dict:
    key_of = jax.random.split(jax.random.key(seed), 14)
    attn_heads = normal_values(key_of[0], (TOKENS, HD_ALL), 1.0, 6.0, ((0, 32), (1, 4)))
    out_weight = normal_values(key_of[1], (HD_ALL, D), HD_ALL ** -0.5, 0.09375, ((0, 4),))
    residual = normal_values(key_of[2], (TOKENS, D), 1.0, 6.0, ((0, 128),))
    norm_gain = jnp.clip(1.0 + 0.18 * jax.random.normal(key_of[3], (D,), jnp.float32), 0.099609375, 1.8984375).astype(jnp.bfloat16)
    shared_gate = normal_values(key_of[4], (D,), D ** -0.5, 0.09375)
    shared_gate_proj = normal_values(key_of[5], (D, FF_SH), D ** -0.5, 0.09375, ((1, 128),))
    shared_up_proj = normal_values(key_of[6], (D, FF_SH), D ** -0.5, 0.09375, ((1, 128),))
    shared_down_proj = normal_values(key_of[7], (FF_SH, D), FF_SH ** -0.5, 0.0390625, ((0, 128),))
    expert_gate = normal_values(key_of[8], (DEVICES, D, HALF), D ** -0.5, 0.09375, ((0, 128),))
    expert_up_weight = normal_values(key_of[9], (DEVICES, D, HALF), D ** -0.5, 0.09375, ((0, 128),))
    expert_down = normal_values(key_of[10], (DEVICES, HALF, D), FF_E ** -0.5, 0.15625, ((0, 128),))
    expert_choice_keys = jax.random.split(jax.random.fold_in(key_of[11], 1), TOKENS // TOK_DEV)
    expert_choice_turns = jax.random.permutation(jax.random.fold_in(key_of[11], 3), TOKENS // TOK_DEV)
    expert_choice = jax.vmap(lambda own, number: routed_block(jax.random.fold_in(key_of[11], 2), own, number, TOK_DEV, EXPERTS, TOP, CAP, 2))(expert_choice_keys, expert_choice_turns).reshape((TOKENS, TOP))
    gate_probs = jnp.clip(jnp.exp(math.log(0.4) - 2.9957323 * jax.random.uniform(key_of[12], (TOKENS, TOP), jnp.float32) ** levels(key_of[12], (TOKENS, TOP), ((0, 128),), -0.2, 0.2)), 0.02, 0.4)
    return dict(attn_heads=attn_heads, out_weight=out_weight, residual=residual, norm_gain=norm_gain, shared_gate=shared_gate, shared_gate_proj=shared_gate_proj, shared_up_proj=shared_up_proj, shared_down_proj=shared_down_proj, expert_gate=expert_gate, expert_up_weight=expert_up_weight, expert_down=expert_down, expert_choice=expert_choice, gate_probs=gate_probs)


def reference(attn_heads, out_weight, residual, norm_gain, shared_gate, shared_gate_proj, shared_up_proj, shared_down_proj, expert_gate, expert_up_weight, expert_down, expert_choice, gate_probs):
    mid = (residual.astype(jnp.float32) + jnp.dot(attn_heads, out_weight, preferred_element_type=jnp.float32)).astype(jnp.bfloat16)
    midf = mid.astype(jnp.float32)
    scale = lax.rsqrt(lax.optimization_barrier(jnp.mean(midf * midf, axis=1, keepdims=True)) + 1e-06)
    normed = (midf * scale * norm_gain.astype(jnp.float32)).astype(jnp.bfloat16)
    share = jax.nn.sigmoid(jnp.dot(normed, shared_gate, preferred_element_type=jnp.float32))
    gate = jnp.dot(normed, shared_gate_proj, preferred_element_type=jnp.float32)
    upper = jnp.dot(normed, shared_up_proj, preferred_element_type=jnp.float32)
    hidden = (jax.nn.silu(gate) * upper).astype(jnp.bfloat16)
    shared_out = jnp.dot(hidden, shared_down_proj, preferred_element_type=jnp.float32)
    chosen = expert_choice.reshape(DEVICES, TOK_DEV, TOP)
    expert_ids = jnp.arange(EXPERTS, dtype=jnp.int32)
    picked = (chosen[..., None] == expert_ids).astype(jnp.int32)
    per_expert = lax.optimization_barrier(jnp.sum(picked, axis=2))
    earlier = jnp.cumsum(per_expert, axis=1) - per_expert
    slot = lax.optimization_barrier(jnp.sum(picked * earlier[:, :, None, :], axis=3)).astype(jnp.int32)
    source = jnp.broadcast_to(jnp.arange(DEVICES, dtype=jnp.int32)[:, None, None], chosen.shape)
    token_row_block = jnp.broadcast_to(normed.reshape(DEVICES, TOK_DEV, 1, D), (DEVICES, TOK_DEV, TOP, D))
    buffer = jnp.zeros((EXPERTS, DEVICES, CAP, D), jnp.bfloat16).at[chosen, source, slot].set(token_row_block)

    def one_expert(index):
        expert_token_rows = buffer[index].reshape(DEVICES * CAP, D)
        total = jnp.zeros((DEVICES * CAP, D), jnp.float32)
        for half in range(2):
            select_where = half * EXPERTS + index
            expert_gate_value = jnp.dot(expert_token_rows, expert_gate[select_where], preferred_element_type=jnp.float32)
            expert_up_value = jnp.dot(expert_token_rows, expert_up_weight[select_where], preferred_element_type=jnp.float32)
            expert_hidden_state = (jax.nn.silu(expert_gate_value) * expert_up_value).astype(jnp.bfloat16)
            part = jnp.dot(expert_hidden_state, expert_down[select_where], preferred_element_type=jnp.float32).astype(jnp.bfloat16)
            total = total + part.astype(jnp.float32)
        return total.reshape(DEVICES, CAP, D)
    outputs = lax.map(one_expert, expert_ids)
    gathered = outputs[chosen, source, slot]
    routed = lax.optimization_barrier(jnp.sum(gate_probs.reshape(DEVICES, TOK_DEV, TOP, 1) * gathered, axis=2)).reshape(TOKENS, D)
    ffn_out = (share[:, None] * shared_out + routed).astype(jnp.bfloat16)
    return (mid, ffn_out)
```

```python
import jax
import jax.numpy as jnp
from jax import lax
from jax.experimental import pallas as pl
from jax.experimental.pallas import tpu as pltpu
from jax.sharding import PartitionSpec as P

MESH = pl.DeviceIdType.MESH
BF = jnp.bfloat16
F32 = jnp.float32
TOK = 8
PAIR = 16
D = 3584
HALF_D = D // 2
WIDTHS = (640, 640, 512)
OFFS = (0, 640, 1280)
CARRY = 640
ORDERS = ((2, 1, 0), (1, 0, 2), (0, 2, 1))
HID = 160
HALF = 640
EXPERTS = 64
CHUNK = 256
SLOTS = 64
N_AG = 3 * (3 + 4 + 6 + 7)
N_RS = 3 * (1 + 6 + 6 + 3)


def silu(v):
    return v / (1.0 + jnp.exp(-v))


def kernel(
    heads, out_w, residual, gain, sgate, sgp, sup, sdn, eg, eu, ed, choice, probs,
    mid_out, ffn_out,
    wo, wsg, wsu, weg, weu, wed, rhs,
    part, sbuf, rz, nx, rx, g,
    place, pslot, share_s, lhs, xe, he,
    s0, s1, s2, t0, t1, t2, u0, u1, u2,
    a0, a1, a2, b0, b1, b2, c0, c1, c2,
    fin, rfin,
    wo_sem, w_sem, zs_sem, zr_sem, x_sem, ags, agr, rss, rsr,
):
    dp = lax.axis_index("dp")
    z0 = lax.axis_index("tensor")
    core = lax.rem(dp, 2)
    other = 1 - core
    pos = (dp // 8, lax.rem(dp // 2, 4), z0)

    def device(y, x, c, z):
        return ((y * 4 + x) * 2 + c, z)

    def near(axis, k):
        return lax.rem(pos[axis] + k, 4)

    def peer(axis, k):
        at = list(pos)
        at[axis] = near(axis, k)
        return device(at[0], at[1], core, at[2])

    sibling = device(pos[0], pos[1], other, pos[2])

    barrier = pltpu.get_barrier_semaphore()
    for axis in range(3):
        for k in range(1, 4):
            pl.semaphore_signal(barrier, inc=1, device_id=peer(axis, k), device_id_type=MESH)
    pl.semaphore_signal(barrier, inc=1, device_id=sibling, device_id_type=MESH)

    def wo_copy(j):
        return pltpu.make_async_copy(
            out_w.at[:, pl.ds(pl.multiple_of(j * 256, 256), 256)], wo.at[j], wo_sem.at[j]
        )

    for j in range(7):
        wo_copy(j).start()
        wo_copy(j + 7).start()
    loads = [
        pltpu.make_async_copy(sgp, wsg, w_sem.at[0]),
        pltpu.make_async_copy(sup, wsu, w_sem.at[1]),
        pltpu.make_async_copy(eg.at[0], weg, w_sem.at[2]),
        pltpu.make_async_copy(eu.at[0], weu, w_sem.at[3]),
        pltpu.make_async_copy(ed.at[0], wed, w_sem.at[4]),
    ]
    for h in range(2):
        for y in range(4):
            loads.append(
                pltpu.make_async_copy(
                    sdn.at[:, pl.ds(h * HALF_D, HALF_D)],
                    rhs.at[h, y, pl.ds(0, HID)],
                    w_sem.at[5 + h * 4 + y],
                )
            )
    for load in loads:
        load.start()

    def project(j, carry):
        wo_copy(j).wait()
        wo_copy(j + 7).wait()
        cols = pl.ds(pl.multiple_of(j * 256, 256), 256)
        left = jnp.dot(heads[...], wo[j], preferred_element_type=F32)
        right = jnp.dot(heads[...], wo[j + 7], preferred_element_type=F32)
        part[0, :, :, cols] = left.reshape(4, TOK, 256)
        part[1, :, :, cols] = right.reshape(4, TOK, 256)
        for q in range(4):
            rows = slice(q * TOK, (q + 1) * TOK)
            sbuf[q, :, cols] = jnp.concatenate([left[rows], right[rows]], axis=0).astype(BF)
        return carry

    lax.fori_loop(0, 7, project, 0)

    pl.semaphore_wait(barrier, 10)

    zc = []
    for k in range(1, 4):
        c = pltpu.make_async_remote_copy(
            src_ref=sbuf.at[near(2, k)], dst_ref=rz.at[k - 1],
            send_sem=zs_sem.at[k - 1], recv_sem=zr_sem.at[k - 1],
            device_id=peer(2, k), device_id_type=MESH,
        )
        c.start()
        zc.append(c)

    rhs[:, :, HID:256, :] = jnp.zeros((2, 4, 256 - HID, HALF_D), BF)

    for c in zc:
        c.wait_recv()

    square = jnp.zeros((TOK, 1), F32)
    mids = []
    for h in range(2):
        cols = slice(h * HALF_D, (h + 1) * HALF_D)
        total = part[h, z0]
        for k in range(3):
            total = total + rz[k].astype(F32)[h * TOK : (h + 1) * TOK]
        mid = (residual[:, cols].astype(F32) + total).astype(BF)
        mid_out[:, cols] = mid
        midf = mid.astype(F32)
        mids.append(midf)
        square = square + jnp.sum(midf * midf, axis=1, keepdims=True)
    scale = lax.rsqrt(square * (1.0 / D) + 1e-06)
    logit = jnp.zeros((TOK, 1), F32)
    for h in range(2):
        cols = slice(h * HALF_D, (h + 1) * HALF_D)
        normed = (mids[h] * scale * gain[:, cols].astype(F32)).astype(BF).astype(F32)
        nx[h, :, 0:HALF_D] = normed
        logit = logit + jnp.sum(normed * sgate[:, cols].astype(F32), axis=1, keepdims=True)
    share = 1.0 / (1.0 + jnp.exp(-logit))

    lane = lax.broadcasted_iota(jnp.int32, (TOK, 128), 1)
    facts = jnp.zeros((TOK, 128), F32)
    chosen = choice[...].astype(F32)
    weight = probs[...]
    high = weight.astype(BF).astype(F32)
    low = weight - high
    for k in range(8):
        facts = jnp.where(lane == k, chosen[:, k : k + 1], facts)
        facts = jnp.where(lane == 8 + k, high[:, k : k + 1], facts)
        facts = jnp.where(lane == 16 + k, low[:, k : k + 1], facts)
    share_high = share.astype(BF).astype(F32)
    facts = jnp.where(lane == 24, share_high, facts)
    facts = jnp.where(lane == 25, share - share_high, facts)
    for h in range(2):
        nx[h, :, HALF_D : HALF_D + 128] = facts

    swap = pltpu.make_async_remote_copy(
        src_ref=nx.at[other], dst_ref=rx, send_sem=x_sem.at[0], recv_sem=x_sem.at[1],
        device_id=sibling, device_id_type=MESH,
    )
    swap.start()
    swap.wait_recv()
    mine = nx[core]
    theirs = rx[...]
    first = core == 0
    block = jnp.concatenate(
        [jnp.where(first, mine, theirs), jnp.where(first, theirs, mine)], axis=0
    ).astype(BF)
    for o in range(3):
        g[core, o, pos[0], pos[1], pos[2]] = block[:, o * CARRY : (o + 1) * CARRY]

    pending = []
    count = [0]

    def gsend(o, at, dev):
        i = count[0]
        count[0] += 1
        ref = g.at[(core, o) + tuple(at)]
        c = pltpu.make_async_remote_copy(
            src_ref=ref, dst_ref=ref, send_sem=ags.at[i], recv_sem=agr.at[i],
            device_id=dev, device_id_type=MESH,
        )
        c.start()
        pending.append(c)
        return c

    def where_(o, first_, second, third):
        at = [None, None, None]
        for axis, v in zip(ORDERS[o], (first_, second, third)):
            at[axis] = v
        return at

    ALL, A, B = pl.ds(0, 4), pl.ds(0, 2), pl.ds(2, 2)
    own = [[pos[axis] for axis in ORDERS[o]] for o in range(3)]

    got = [[gsend(o, pos, peer(ORDERS[o][0], k)) for k in range(1, 4)] for o in range(3)]
    stage = []
    for o in range(3):
        for c in got[o]:
            c.wait_recv()
        mine_at = where_(o, ALL, own[o][1], own[o][2])
        ax = ORDERS[o][1]
        stage.append((gsend(o, mine_at, peer(ax, 1)), gsend(o, mine_at, peer(ax, 3))))
    hop = []
    for o in range(3):
        ax = ORDERS[o][1]
        stage[o][0].wait_recv()
        f1 = gsend(o, where_(o, A, near(ax, 3), own[o][2]), peer(ax, 1))
        stage[o][1].wait_recv()
        f2 = gsend(o, where_(o, B, near(ax, 1), own[o][2]), peer(ax, 3))
        hop.append((f1, f2))
    stage = []
    sib = []
    for o in range(3):
        for c in hop[o]:
            c.wait_recv()
        ax = ORDERS[o][2]
        at_a = where_(o, A, ALL, own[o][2])
        at_b = where_(o, B, ALL, own[o][2])
        ra = gsend(o, at_a, peer(ax, 1))
        lb = gsend(o, at_b, peer(ax, 3))
        rb = gsend(o, at_b, peer(ax, 1))
        la = gsend(o, at_a, peer(ax, 3))
        stage.append((ra, lb, rb, la))
        sib.append(gsend(o, where_(o, ALL, ALL, own[o][2]), sibling))
    hop = [[], [], []]
    for event in range(4):
        for o in range(3):
            ax = ORDERS[o][2]
            half = (A, B, B, A)[event]
            came = near(ax, (3, 1, 3, 1)[event])
            at = where_(o, half, ALL, came)
            stage[o][event].wait_recv()
            if event < 2:
                hop[o].append(gsend(o, at, peer(ax, (1, 3)[event])))
            sib.append(gsend(o, at, sibling))
    for event in range(2):
        for o in range(3):
            ax = ORDERS[o][2]
            hop[o][event].wait_recv()
            sib.append(gsend(o, where_(o, (A, B)[event], ALL, near(ax, 2)), sibling))
    for c in sib:
        c.wait_recv()

    expert = lax.rem(dp * 4 + z0, EXPERTS).astype(F32)
    told = g[0, 2, :, :, :, :, 512:640].reshape(1024, 128).astype(F32)
    share_s[...] = jnp.broadcast_to(told[:, 24:25] + told[:, 25:26], (1024, 128))
    turned = told.T
    hit8 = turned[0:8] == expert
    p_row = jnp.sum(jnp.where(hit8, turned[8:16] + turned[16:24], 0.0), axis=0, keepdims=True)
    hit = jnp.sum(jnp.where(hit8, 1.0, 0.0), axis=0, keepdims=True)
    hit = jnp.broadcast_to(hit, (8, 1024))
    token = lax.broadcasted_iota(jnp.int32, (8, 1024), 1)
    rank = jnp.zeros((8, 1024), F32)
    for k in range(1, 8):
        rank = rank + jnp.where(lax.rem(token, 8) >= k, pltpu.roll(hit, k, axis=1), 0.0)
    row = (lax.rem(token // 8, 32) * 2).astype(F32) + rank
    row = jnp.where(hit > 0.5, row, -1000.0)
    row1 = row[0:1]
    column = jnp.broadcast_to(row1, (128, 1024)).T
    lane1 = lax.broadcasted_iota(jnp.int32, (1024, 128), 1).astype(F32)
    lhs[:, :, 0:128] = jnp.zeros((4, CHUNK, 128), BF)
    lhs[:, :, 128:256] = (
        jnp.where(lane1 - (HID - 128.0) == column, 1.0, 0.0).astype(BF).reshape(4, CHUNK, 128)
    )
    slot_id = lax.broadcasted_iota(jnp.int32, (SLOTS, CHUNK), 0).astype(F32)
    for y in range(4):
        cols = slice(y * CHUNK, (y + 1) * CHUNK)
        chosen_y = jnp.where(slot_id == row1[:, cols], 1.0, 0.0)
        place[y] = chosen_y.astype(BF)
        pslot[pl.ds(y * SLOTS, SLOTS)] = jnp.broadcast_to(
            jnp.sum(chosen_y * p_row[:, cols], axis=1, keepdims=True), (SLOTS, 128)
        )

    loads[0].wait()
    loads[1].wait()

    def hidden(y, carry):
        x = jnp.concatenate(
            [
                g[h, o, y].reshape(CHUNK, CARRY)[:, : WIDTHS[o]]
                for h in range(2)
                for o in range(3)
            ],
            axis=1,
        )
        xe[pl.ds(pl.multiple_of(y * SLOTS, SLOTS), SLOTS)] = jnp.dot(
            place[y], x, preferred_element_type=F32
        ).astype(BF)
        gate = jnp.dot(x, wsg[...], preferred_element_type=F32)
        upper = jnp.dot(x, wsu[...], preferred_element_type=F32)
        share_y = share_s[pl.ds(pl.multiple_of(y * CHUNK, CHUNK), CHUNK)]
        hs = silu(gate) * upper
        lhs[y, :, 0:128] = (hs[:, 0:128] * share_y).astype(BF)
        lhs[y, :, 128:HID] = (hs[:, 128:HID] * share_y[:, 0 : HID - 128]).astype(BF)
        return carry

    lax.fori_loop(0, 4, hidden, 0)

    loads[2].wait()
    loads[3].wait()

    def expert_hidden(i, carry):
        cols = pl.ds(pl.multiple_of(i * 128, 128), 128)
        w = jnp.concatenate([weg[:, cols], weu[:, cols]], axis=1)
        r = jnp.dot(xe[...], w, preferred_element_type=F32)
        he[:, cols] = (silu(r[:, 0:128]) * r[:, 128:256]).astype(BF)
        return carry

    lax.fori_loop(0, HALF // 128, expert_hidden, 0)

    for load in loads[4:]:
        load.wait()

    def expert_down(i, carry):
        h = i // 7
        j = lax.rem(i, 7)
        r = jnp.dot(
            he[...], wed[:, pl.ds(pl.multiple_of(i * 256, 256), 256)], preferred_element_type=F32
        )
        by = pslot[...]
        r = (r * jnp.concatenate([by, by], axis=1)).astype(BF)
        cols = pl.ds(pl.multiple_of(j * 256, 256), 256)
        for y in range(4):
            rhs[h, y, pl.ds(HID, SLOTS), cols] = r[y * SLOTS : (y + 1) * SLOTS]
        return carry

    lax.fori_loop(0, 14, expert_down, 0)

    s, t, u = (s0, s1, s2), (t0, t1, t2), (u0, u1, u2)
    half_in = (a0, a1, a2)
    full_in = (b0, b1, b2)
    last_in = (c0, c1, c2)
    count[0] = 0

    def rsend(src, dst, dev):
        i = count[0]
        count[0] += 1
        c = pltpu.make_async_remote_copy(
            src_ref=src, dst_ref=dst, send_sem=rss.at[i], recv_sem=rsr.at[i],
            device_id=dev, device_id_type=MESH,
        )
        c.start()
        pending.append(c)
        return c

    def combine(o, h, to):
        cols = pl.ds(OFFS[o], WIDTHS[o])

        def step(y, carry):
            r = jnp.dot(lhs[y], rhs[h, y, :, cols], preferred_element_type=F32)
            to[y] = r.astype(BF).reshape(4, 4, PAIR, WIDTHS[o])
            return carry

        lax.fori_loop(0, 4, step, 0)

    sib = []
    for o in range(3):
        combine(o, other, t[o])
        sib.append(rsend(t[o], u[o], sibling))
    for o in range(3):
        combine(o, core, s[o])

    def at1(o, c, half):
        ax = ORDERS[o][2]
        rest = [half, ALL]
        return tuple(c if axis == ax else rest.pop(0) for axis in range(3))

    def add_first(o, c, lo, hi, terms):
        ax = ORDERS[o][2]

        def step(i, carry):
            rest = [i, ALL]
            at = tuple(c if axis == ax else rest.pop(0) for axis in range(3))
            total = s[o][at].astype(F32)
            for term, base in terms:
                total = total + term[i - base].astype(F32)
            s[o][at] = total.astype(BF)
            return carry

        lax.fori_loop(lo, hi, step, 0)

    stage = []
    for o in range(3):
        sib[o].wait_recv()

        def step(i, carry, o=o):
            y = i // 4
            x = lax.rem(i, 4)
            s[o][y, x] = (s[o][y, x].astype(F32) + u[o][y, x].astype(F32)).astype(BF)
            return carry

        lax.fori_loop(0, 16, step, 0)
        ax = ORDERS[o][2]
        so, ha, fu = s[o], half_in[o], full_in[o]
        c1_ = rsend(so.at[at1(o, near(ax, 2), A)], ha.at[0], peer(ax, 1))
        c4_ = rsend(so.at[at1(o, near(ax, 2), B)], ha.at[1], peer(ax, 3))
        c2_ = rsend(so.at[at1(o, near(ax, 1), B)], fu.at[0, B], peer(ax, 1))
        c5_ = rsend(so.at[at1(o, near(ax, 3), A)], fu.at[1, A], peer(ax, 3))
        stage.append([c1_, c4_, c2_, c5_])
    for o in range(3):
        ax = ORDERS[o][2]
        so, ha, fu = s[o], half_in[o], full_in[o]
        stage[o][0].wait_recv()
        add_first(o, near(ax, 1), 0, 2, [(ha.at[0], 0)])
        stage[o].append(rsend(so.at[at1(o, near(ax, 1), A)], fu.at[0, A], peer(ax, 1)))
        stage[o][1].wait_recv()
        add_first(o, near(ax, 3), 2, 4, [(ha.at[1], 2)])
        stage[o].append(rsend(so.at[at1(o, near(ax, 3), B)], fu.at[1, B], peer(ax, 3)))

    def at2(o, c, half):
        return tuple(where_(o, half, c, own[o][2]))

    stage2 = []
    for o in range(3):
        for c in stage[o][2:]:
            c.wait_recv()
        add_first(o, own[o][2], 0, 4, [(full_in[o].at[0], 0), (full_in[o].at[1], 0)])
        ax = ORDERS[o][1]
        so, la = s[o], last_in[o]
        c1_ = rsend(so.at[at2(o, near(ax, 2), A)], la.at[pl.ds(0, 2)], peer(ax, 1))
        c4_ = rsend(so.at[at2(o, near(ax, 2), B)], la.at[pl.ds(2, 2)], peer(ax, 3))
        c2_ = rsend(so.at[at2(o, near(ax, 1), B)], la.at[pl.ds(6, 2)], peer(ax, 1))
        c5_ = rsend(so.at[at2(o, near(ax, 3), A)], la.at[pl.ds(8, 2)], peer(ax, 3))
        stage2.append([c1_, c4_, c2_, c5_])
    for o in range(3):
        ax = ORDERS[o][1]
        so, la = s[o], last_in[o]
        stage2[o][0].wait_recv()
        at = at2(o, near(ax, 1), A)
        so[at] = (so[at].astype(F32) + la[0:2].astype(F32)).astype(BF)
        stage2[o].append(rsend(so.at[at], la.at[pl.ds(4, 2)], peer(ax, 1)))
        stage2[o][1].wait_recv()
        at = at2(o, near(ax, 3), B)
        so[at] = (so[at].astype(F32) + la[2:4].astype(F32)).astype(BF)
        stage2[o].append(rsend(so.at[at], la.at[pl.ds(10, 2)], peer(ax, 3)))

    stage3 = []
    for o in range(3):
        for c in stage2[o][2:]:
            c.wait_recv()
        so, la = s[o], last_in[o]
        at = at2(o, own[o][1], ALL)
        so[at] = (
            so[at].astype(F32) + la[4:8].astype(F32) + la[8:12].astype(F32)
        ).astype(BF)
        ax = ORDERS[o][0]
        stage3.append(
            [
                rsend(
                    so.at[tuple(where_(o, near(ax, k), own[o][1], own[o][2]))],
                    la.at[11 + k],
                    peer(ax, k),
                )
                for k in range(1, 4)
            ]
        )
    for o in range(3):
        total = s[o][pos].astype(F32)
        for k in range(3):
            stage3[o][k].wait_recv()
            total = total + last_in[o][12 + k].astype(F32)
        cols = pl.ds(OFFS[o], WIDTHS[o])
        fin[0, :, cols] = total[0:TOK]
        fin[1, :, cols] = total[TOK:PAIR]

    swap_back = pltpu.make_async_remote_copy(
        src_ref=fin.at[other], dst_ref=rfin, send_sem=x_sem.at[2], recv_sem=x_sem.at[3],
        device_id=sibling, device_id_type=MESH,
    )
    swap_back.start()
    swap_back.wait_recv()
    mine = fin[core]
    theirs = rfin[...]
    ffn_out[:, 0:HALF_D] = jnp.where(first, mine, theirs).astype(BF)
    ffn_out[:, HALF_D:D] = jnp.where(first, theirs, mine).astype(BF)

    for c in zc:
        c.wait_send()
    swap.wait_send()
    swap_back.wait_send()
    for c in pending:
        c.wait_send()


def on_device(
    attn_heads, out_weight, residual, norm_gain, shared_gate, shared_gate_proj, shared_up_proj,
    shared_down_proj, expert_gate, expert_up_weight, expert_down, expert_choice, gate_probs,
):
    vm = pl.BlockSpec(memory_space=pltpu.VMEM)
    hbm = pl.BlockSpec(memory_space=pl.ANY)
    V = pltpu.VMEM
    dma = pltpu.SemaphoreType.DMA
    scratch = [
        V((14, 896, 256), BF), V((D, HID), BF), V((D, HID), BF),
        V((D, HALF), BF), V((D, HALF), BF), V((HALF, D), BF), V((2, 4, 256, HALF_D), BF),
        V((2, 4, TOK, HALF_D), F32), V((4, PAIR, HALF_D), BF), V((3, PAIR, HALF_D), BF),
        V((2, TOK, HALF_D + 128), F32), V((TOK, HALF_D + 128), F32),
        V((2, 3, 4, 4, 4, PAIR, CARRY), BF),
        V((4, SLOTS, CHUNK), BF), V((4 * SLOTS, 128), F32), V((1024, 128), F32),
        V((4, CHUNK, 256), BF), V((4 * SLOTS, D), BF), V((4 * SLOTS, HALF), BF),
    ]
    for _ in range(3):
        scratch += [V((4, 4, 4, PAIR, w), BF) for w in WIDTHS]
    scratch += [V((2, 2, 4, PAIR, w), BF) for w in WIDTHS]
    scratch += [V((2, 4, 4, PAIR, w), BF) for w in WIDTHS]
    scratch += [V((15, PAIR, w), BF) for w in WIDTHS]
    scratch += [V((2, TOK, HALF_D), F32), V((TOK, HALF_D), F32)]
    scratch += [
        dma((14,)), dma((13,)), dma((3,)), dma((3,)), dma((4,)),
        dma((N_AG,)), dma((N_AG,)), dma((N_RS,)), dma((N_RS,)),
    ]
    row = jax.ShapeDtypeStruct((TOK, D), BF)
    return pl.pallas_call(
        kernel,
        out_shape=(row, row),
        in_specs=[vm, hbm, vm, vm, vm, hbm, hbm, hbm, hbm, hbm, hbm, vm, vm],
        out_specs=(vm, vm),
        scratch_shapes=scratch,
        compiler_params=pltpu.CompilerParams(
            collective_id=0, has_side_effects=True, vmem_limit_bytes=63 * 1024 * 1024
        ),
    )(
        attn_heads, out_weight, residual, norm_gain.reshape(1, D), shared_gate.reshape(1, D),
        shared_gate_proj, shared_up_proj, shared_down_proj, expert_gate, expert_up_weight,
        expert_down, expert_choice, gate_probs,
    )


def solution(mesh):
    both = ("dp", "tensor")
    in_specs = (
        P("dp", "tensor"), P("tensor", None), P(both, None), P(), P(),
        P(None, both), P(None, both), P(both, None),
        P(both, None, None), P(both, None, None), P(both, None, None),
        P(both, None), P(both, None),
    )
    out_specs = (P(both, None), P(both, None))
    return jax.shard_map(
        on_device, mesh=mesh, in_specs=in_specs, out_specs=out_specs, check_vma=False
    )
```

```python
import jax
import jax.numpy as jnp
from jax import lax
from jax.experimental import pallas as pl
from jax.experimental.pallas import tpu as pltpu
from jax.sharding import PartitionSpec as P

MESH = pl.DeviceIdType.MESH
BF = jnp.bfloat16
F32 = jnp.float32
TOK = 8
PAIR = 16
D = 3584
HALF_D = D // 2
WIDTHS = (640, 640, 512)
OFFS = (0, 640, 1280)
CARRY = 640
ORDERS = ((2, 1, 0), (1, 0, 2), (0, 2, 1))
HID = 160
HALF = 640
EXPERTS = 64
CHUNK = 256
SLOTS = 64
N_AG = 3 * (3 + 3 + 6 + 7)
N_RS = 3 * (4 + 6 + 3 + 3)


def silu(v):
    return v / (1.0 + jnp.exp(-v))


def kernel(
    heads, out_w, residual, gain, sgate, sgp, sup, sdn, eg, eu, ed, choice, probs,
    both_out,
    wo, wsg, wsu, weg, weu, wed, rhs,
    part, sbuf, rz, nx, rx, g,
    acc_g, acc_u, place, pslot, share_s, lhs, xe, he,
    s0, s1, s2, t0, t1, t2, u0, u1, u2,
    a0, a1, a2, b0, b1, b2, c0, c1, c2, d0, d1, d2,
    fin, rfin,
    w_sem, again_sem, zs_sem, zr_sem, x_sem, ags, agr, rss, rsr,
):
    dp = lax.axis_index("dp")
    z0 = lax.axis_index("tensor")
    core = lax.rem(dp, 2)
    other = 1 - core
    pos = (dp // 8, lax.rem(dp // 2, 4), z0)

    def device(y, x, c, z):
        return ((y * 4 + x) * 2 + c, z)

    def near(axis, k):
        return lax.rem(pos[axis] + k, 4)

    def peer(axis, k):
        at = list(pos)
        at[axis] = near(axis, k)
        return device(at[0], at[1], core, at[2])

    sibling = device(pos[0], pos[1], other, pos[2])

    wo_load = pltpu.make_async_copy(out_w, wo, w_sem.at[0])
    loads = [
        pltpu.make_async_copy(sgp, wsg, w_sem.at[1]),
        pltpu.make_async_copy(sup, wsu, w_sem.at[2]),
        pltpu.make_async_copy(eg.at[0], weg, w_sem.at[3]),
        pltpu.make_async_copy(eu.at[0], weu, w_sem.at[4]),
        pltpu.make_async_copy(ed.at[0], wed, w_sem.at[5]),
    ]
    for h in range(2):
        cols = pl.ds(h * HALF_D, HALF_D)
        loads.append(
            pltpu.make_async_copy(sdn.at[:, cols], rhs.at[h, 0, pl.ds(0, HID)], w_sem.at[6 + h])
        )
    wo_load.start()
    for load in loads[0:4]:
        load.start()

    barrier = pltpu.get_barrier_semaphore()
    for axis in range(3):
        for k in range(1, 4):
            pl.semaphore_signal(barrier, inc=1, device_id=peer(axis, k), device_id_type=MESH)
    pl.semaphore_signal(barrier, inc=1, device_id=sibling, device_id_type=MESH)

    def project(j, carry):
        at = pl.multiple_of(j * 256, 256)
        cols = pl.ds(at, 256)
        left = jnp.dot(heads[...], wo[:, cols], preferred_element_type=F32)
        right = jnp.dot(
            heads[...], wo[:, pl.ds(at + HALF_D, 256)], preferred_element_type=F32
        )
        part[0, :, :, cols] = left.reshape(4, TOK, 256)
        part[1, :, :, cols] = right.reshape(4, TOK, 256)
        for q in range(4):
            rows = slice(q * TOK, (q + 1) * TOK)
            sbuf[q, :, cols] = jnp.concatenate([left[rows], right[rows]], axis=0).astype(BF)
        return carry

    wo_load.wait()
    lax.fori_loop(0, 7, project, 0)

    pl.semaphore_wait(barrier, 10)

    zc = []
    for k in range(1, 4):
        c = pltpu.make_async_remote_copy(
            src_ref=sbuf.at[near(2, k)], dst_ref=rz.at[k - 1],
            send_sem=zs_sem.at[k - 1], recv_sem=zr_sem.at[k - 1],
            device_id=peer(2, k), device_id_type=MESH,
        )
        c.start()
        zc.append(c)

    rhs[:, :, HID:256, :] = jnp.zeros((2, 4, 256 - HID, HALF_D), BF)

    for c in zc:
        c.wait_recv()

    square = jnp.zeros((TOK, 1), F32)
    mids = []
    for h in range(2):
        cols = slice(h * HALF_D, (h + 1) * HALF_D)
        total = part[h, z0]
        for k in range(3):
            total = total + rz[k].astype(F32)[h * TOK : (h + 1) * TOK]
        mid = (residual[:, cols].astype(F32) + total).astype(BF)
        both_out[0, :, cols] = mid
        midf = mid.astype(F32)
        mids.append(midf)
        square = square + jnp.sum(midf * midf, axis=1, keepdims=True)
    scale = lax.rsqrt(square * (1.0 / D) + 1e-06)
    logit = jnp.zeros((TOK, 1), F32)
    for h in range(2):
        cols = slice(h * HALF_D, (h + 1) * HALF_D)
        normed = (mids[h] * scale * gain[cols].astype(F32).reshape(1, HALF_D)).astype(BF).astype(F32)
        nx[h, :, 0:HALF_D] = normed
        logit = logit + jnp.sum(normed * sgate[cols].astype(F32).reshape(1, HALF_D), axis=1, keepdims=True)
    share = 1.0 / (1.0 + jnp.exp(-logit))

    lane = lax.broadcasted_iota(jnp.int32, (TOK, 128), 1)
    facts = jnp.zeros((TOK, 128), F32)
    chosen = choice[...].astype(F32)
    weight = probs[...]
    high = weight.astype(BF).astype(F32)
    low = weight - high
    for k in range(8):
        facts = jnp.where(lane == k, chosen[:, k : k + 1], facts)
        facts = jnp.where(lane == 8 + k, high[:, k : k + 1], facts)
        facts = jnp.where(lane == 16 + k, low[:, k : k + 1], facts)
    share_high = share.astype(BF).astype(F32)
    facts = jnp.where(lane == 24, share_high, facts)
    facts = jnp.where(lane == 25, share - share_high, facts)
    for h in range(2):
        nx[h, :, HALF_D : HALF_D + 128] = facts

    swap = pltpu.make_async_remote_copy(
        src_ref=nx.at[other], dst_ref=rx, send_sem=x_sem.at[0], recv_sem=x_sem.at[1],
        device_id=sibling, device_id_type=MESH,
    )
    swap.start()
    swap.wait_recv()
    mine = nx[core]
    theirs = rx[...]
    first = core == 0
    block = jnp.concatenate(
        [jnp.where(first, mine, theirs), jnp.where(first, theirs, mine)], axis=0
    ).astype(BF)
    for o in range(3):
        g[core, o, pos[0], pos[1], pos[2]] = block[:, o * CARRY : (o + 1) * CARRY]

    again = []
    for h in range(2):
        for y in range(1, 4):
            again.append(
                pltpu.make_async_copy(
                    rhs.at[h, 0, pl.ds(0, HID)], rhs.at[h, y, pl.ds(0, HID)],
                    again_sem.at[h * 3 + y - 1],
                )
            )

    pending = []
    count = [0]

    def gsend(o, at, dev):
        i = count[0]
        count[0] += 1
        ref = g.at[(core, o) + tuple(at)]
        c = pltpu.make_async_remote_copy(
            src_ref=ref, dst_ref=ref, send_sem=ags.at[i], recv_sem=agr.at[i],
            device_id=dev, device_id_type=MESH,
        )
        c.start()
        pending.append(c)
        return c

    def where_(o, first_, second, third):
        at = [None, None, None]
        for axis, v in zip(ORDERS[o], (first_, second, third)):
            at[axis] = v
        return at

    ALL, A, B = pl.ds(0, 4), pl.ds(0, 2), pl.ds(2, 2)
    own = [[pos[axis] for axis in ORDERS[o]] for o in range(3)]

    got = [[gsend(o, pos, peer(ORDERS[o][0], k)) for k in (1, 3, 2)] for o in range(3)]
    for load in loads[4:]:
        load.start()
    acc_g[...] = jnp.zeros((4, 4, 4, PAIR, HID), F32)
    acc_u[...] = jnp.zeros((4, 4, 4, PAIR, HID), F32)
    for load in loads[0:4]:
        load.wait()

    def absorb(h, o, k):
        at = tuple(where_(o, ALL, ALL, near(ORDERS[o][2], k)))
        x = g[(h, o) + at].reshape(CHUNK, CARRY)[:, : WIDTHS[o]]
        cols = pl.ds(pl.multiple_of(h * HALF_D + OFFS[o], 128), WIDTHS[o])
        turn = (((1,), (1,)), ((), ()))
        for acc, w in ((acc_g, wsg), (acc_u, wsu)):
            r = lax.dot_general(x, w[:, cols], turn, preferred_element_type=F32)
            acc[at] = acc[at] + r.reshape(4, 4, PAIR, HID)

    hop = []
    for o in range(3):
        for c in got[o]:
            c.wait_recv()
        mine_at = where_(o, ALL, own[o][1], own[o][2])
        hop.append([gsend(o, mine_at, peer(ORDERS[o][1], k)) for k in (1, 3, 2)])
    for load in loads[4:]:
        load.wait()
    for copy in again:
        copy.start()
    stage = []
    sib = [[], [], []]
    for o in range(3):
        for c in hop[o]:
            c.wait_recv()
        ax = ORDERS[o][2]
        at_a = where_(o, A, ALL, own[o][2])
        at_b = where_(o, B, ALL, own[o][2])
        ra = gsend(o, at_a, peer(ax, 1))
        lb = gsend(o, at_b, peer(ax, 3))
        rb = gsend(o, at_b, peer(ax, 1))
        la = gsend(o, at_a, peer(ax, 3))
        stage.append((ra, lb, rb, la))
        sib[o].append(gsend(o, where_(o, ALL, ALL, own[o][2]), sibling))
    for o in range(3):
        absorb(core, o, 0)
    for o in range(3):
        sib[o][0].wait_recv()
        absorb(other, o, 0)
    hop = [[], [], []]
    for event in range(4):
        for o in range(3):
            ax = ORDERS[o][2]
            half = (A, B, B, A)[event]
            came = near(ax, (3, 1, 3, 1)[event])
            at = where_(o, half, ALL, came)
            stage[o][event].wait_recv()
            if event < 2:
                hop[o].append(gsend(o, at, peer(ax, (1, 3)[event])))
            sib[o].append(gsend(o, at, sibling))
    for o in range(3):
        absorb(core, o, 3)
        absorb(core, o, 1)
    for o in range(3):
        sib[o][1].wait_recv()
        sib[o][3].wait_recv()
        absorb(other, o, 3)
        sib[o][2].wait_recv()
        sib[o][4].wait_recv()
        absorb(other, o, 1)
    for event in range(2):
        for o in range(3):
            ax = ORDERS[o][2]
            hop[o][event].wait_recv()
            sib[o].append(gsend(o, where_(o, (A, B)[event], ALL, near(ax, 2)), sibling))
    for o in range(3):
        absorb(core, o, 2)
    for o in range(3):
        sib[o][5].wait_recv()
        sib[o][6].wait_recv()
        absorb(other, o, 2)

    expert = lax.rem(dp * 4 + z0, EXPERTS).astype(F32)
    told = g[0, 2, :, :, :, :, 512:640].reshape(1024, 128).astype(F32)
    share_s[...] = jnp.broadcast_to(told[:, 24:25] + told[:, 25:26], (1024, 128))
    turned = told.T
    hit8 = turned[0:8] == expert
    p_row = jnp.sum(jnp.where(hit8, turned[8:16] + turned[16:24], 0.0), axis=0, keepdims=True)
    hit = jnp.sum(jnp.where(hit8, 1.0, 0.0), axis=0, keepdims=True)
    hit = jnp.broadcast_to(hit, (8, 1024))
    token = lax.broadcasted_iota(jnp.int32, (8, 1024), 1)
    rank = jnp.zeros((8, 1024), F32)
    for k in range(1, 8):
        rank = rank + jnp.where(lax.rem(token, 8) >= k, pltpu.roll(hit, k, axis=1), 0.0)
    row = (lax.rem(token // 8, 32) * 2).astype(F32) + rank
    row = jnp.where(hit > 0.5, row, -1000.0)
    row1 = row[0:1]
    column = jnp.broadcast_to(row1, (128, 1024)).T
    lane1 = lax.broadcasted_iota(jnp.int32, (1024, 128), 1).astype(F32)
    lhs[:, :, 0:128] = jnp.zeros((4, CHUNK, 128), BF)
    lhs[:, :, 128:256] = (
        jnp.where(lane1 - (HID - 128.0) == column, 1.0, 0.0).astype(BF).reshape(4, CHUNK, 128)
    )
    slot_id = lax.broadcasted_iota(jnp.int32, (SLOTS, CHUNK), 0).astype(F32)
    for y in range(4):
        cols = slice(y * CHUNK, (y + 1) * CHUNK)
        chosen_y = jnp.where(slot_id == row1[:, cols], 1.0, 0.0)
        place[y] = chosen_y.astype(BF)
        pslot[pl.ds(y * SLOTS, SLOTS)] = jnp.broadcast_to(
            jnp.sum(chosen_y * p_row[:, cols], axis=1, keepdims=True), (SLOTS, 128)
        )

    def hidden(y, carry):
        x = jnp.concatenate(
            [
                g[h, o, y].reshape(CHUNK, CARRY)[:, : WIDTHS[o]]
                for h in range(2)
                for o in range(3)
            ],
            axis=1,
        )
        xe[pl.ds(pl.multiple_of(y * SLOTS, SLOTS), SLOTS)] = jnp.dot(
            place[y], x, preferred_element_type=F32
        ).astype(BF)
        share_y = share_s[pl.ds(pl.multiple_of(y * CHUNK, CHUNK), CHUNK)]
        hs = silu(acc_g[y].reshape(CHUNK, HID)) * acc_u[y].reshape(CHUNK, HID)
        lhs[y, :, 0:128] = (hs[:, 0:128] * share_y).astype(BF)
        lhs[y, :, 128:HID] = (hs[:, 128:HID] * share_y[:, 0 : HID - 128]).astype(BF)
        return carry

    lax.fori_loop(0, 4, hidden, 0, unroll=True)

    def expert_hidden(i, carry):
        cols = pl.ds(pl.multiple_of(i * 128, 128), 128)
        w = jnp.concatenate([weg[:, cols], weu[:, cols]], axis=1)
        r = jnp.dot(xe[...], w, preferred_element_type=F32)
        he[:, cols] = (silu(r[:, 0:128]) * r[:, 128:256]).astype(BF)
        return carry

    lax.fori_loop(0, HALF // 128, expert_hidden, 0, unroll=True)

    for copy in again:
        copy.wait()

    by = jnp.concatenate([pslot[...]] * 4, axis=1)
    for h in range(2):
        for at, w in ((0, 512), (512, 512), (1024, 512), (1536, 256)):
            r = jnp.dot(
                he[...], wed[:, h * HALF_D + at : h * HALF_D + at + w], preferred_element_type=F32
            )
            r = (r * by[:, 0:w]).astype(BF)
            for y in range(4):
                rhs[h, y, HID : HID + SLOTS, at : at + w] = r[y * SLOTS : (y + 1) * SLOTS]

    s, t, u = (s0, s1, s2), (t0, t1, t2), (u0, u1, u2)
    half_in = (a0, a1, a2)
    full_in = (b0, b1, b2)
    last_in = (c0, c1, c2)
    one_in = (d0, d1, d2)
    count[0] = 0

    def rsend(src, dst, dev):
        i = count[0]
        count[0] += 1
        c = pltpu.make_async_remote_copy(
            src_ref=src, dst_ref=dst, send_sem=rss.at[i], recv_sem=rsr.at[i],
            device_id=dev, device_id_type=MESH,
        )
        c.start()
        pending.append(c)
        return c

    def combine(o, h, to):
        cols = slice(OFFS[o], OFFS[o] + WIDTHS[o])
        for y in range(4):
            r = jnp.dot(lhs[y], rhs[h, y, :, cols], preferred_element_type=F32)
            to[y] = r.astype(BF).reshape(4, 4, PAIR, WIDTHS[o])

    def at1(o, c, half):
        rest = [half, ALL]
        return tuple(c if axis == ORDERS[o][2] else rest.pop(0) for axis in range(3))

    def add1(o, c, lo, hi, terms):
        def step(i, carry):
            at = at1(o, c, i)
            total = s[o][at].astype(F32) + u[o][at].astype(F32)
            for term, base in terms:
                total = total + term[i - base].astype(F32)
            s[o][at] = total.astype(BF)
            return carry

        lax.fori_loop(lo, hi, step, 0)

    for o in range(3):
        combine(o, other, t[o])
    sib = [[], [], []]
    for k in (2, 1, 3, 0):
        for o in range(3):
            at = at1(o, near(ORDERS[o][2], k), ALL)
            sib[o].append(rsend(t[o].at[at], u[o].at[at], sibling))
    for o in range(3):
        combine(o, core, s[o])

    stage = [[], [], []]
    for o in range(3):
        ax = ORDERS[o][2]
        c = near(ax, 2)
        sib[o][0].wait_recv()
        add1(o, c, 0, 2, [])
        stage[o].append(rsend(s[o].at[at1(o, c, A)], half_in[o].at[0], peer(ax, 1)))
        add1(o, c, 2, 4, [])
        stage[o].append(rsend(s[o].at[at1(o, c, B)], half_in[o].at[1], peer(ax, 3)))
    for o in range(3):
        ax = ORDERS[o][2]
        c = near(ax, 1)
        sib[o][1].wait_recv()
        add1(o, c, 2, 4, [])
        stage[o].append(rsend(s[o].at[at1(o, c, B)], full_in[o].at[0, B], peer(ax, 1)))
        c = near(ax, 3)
        sib[o][2].wait_recv()
        add1(o, c, 0, 2, [])
        stage[o].append(rsend(s[o].at[at1(o, c, A)], full_in[o].at[1, A], peer(ax, 3)))
    for o in range(3):
        ax = ORDERS[o][2]
        c = near(ax, 1)
        stage[o][0].wait_recv()
        add1(o, c, 0, 2, [(half_in[o].at[0], 0)])
        stage[o].append(rsend(s[o].at[at1(o, c, A)], full_in[o].at[0, A], peer(ax, 1)))
        c = near(ax, 3)
        stage[o][1].wait_recv()
        add1(o, c, 2, 4, [(half_in[o].at[1], 2)])
        stage[o].append(rsend(s[o].at[at1(o, c, B)], full_in[o].at[1, B], peer(ax, 3)))

    def at2(o, c):
        return tuple(where_(o, ALL, c, own[o][2]))

    stage2 = []
    for o in range(3):
        sib[o][3].wait_recv()
        for c in stage[o][2:]:
            c.wait_recv()
        add1(o, own[o][2], 0, 4, [(full_in[o].at[0], 0), (full_in[o].at[1], 0)])
        ax = ORDERS[o][1]
        stage2.append(
            [
                rsend(s[o].at[at2(o, near(ax, k))], last_in[o].at[k - 1], peer(ax, k))
                for k in (1, 3, 2)
            ]
        )

    stage3 = []
    for o in range(3):
        for c in stage2[o]:
            c.wait_recv()
        at = at2(o, own[o][1])
        total = s[o][at].astype(F32)
        for k in range(3):
            total = total + last_in[o][k].astype(F32)
        s[o][at] = total.astype(BF)
        ax = ORDERS[o][0]
        stage3.append(
            [
                rsend(
                    s[o].at[tuple(where_(o, near(ax, k), own[o][1], own[o][2]))],
                    one_in[o].at[k - 1],
                    peer(ax, k),
                )
                for k in (1, 2, 3)
            ]
        )
    for o in range(3):
        total = s[o][pos].astype(F32)
        for k in range(3):
            stage3[o][k].wait_recv()
            total = total + one_in[o][k].astype(F32)
        cols = pl.ds(OFFS[o], WIDTHS[o])
        fin[0, :, cols] = total[0:TOK]
        fin[1, :, cols] = total[TOK:PAIR]

    swap_back = pltpu.make_async_remote_copy(
        src_ref=fin.at[other], dst_ref=rfin, send_sem=x_sem.at[2], recv_sem=x_sem.at[3],
        device_id=sibling, device_id_type=MESH,
    )
    swap_back.start()
    swap_back.wait_recv()
    mine = fin[core]
    theirs = rfin[...]
    both_out[1, :, 0:HALF_D] = jnp.where(first, mine, theirs).astype(BF)
    both_out[1, :, HALF_D:D] = jnp.where(first, theirs, mine).astype(BF)

    for c in zc:
        c.wait_send()
    swap.wait_send()
    swap_back.wait_send()
    for c in pending:
        c.wait_send()


def on_device(
    attn_heads, out_weight, residual, norm_gain, shared_gate, shared_gate_proj, shared_up_proj,
    shared_down_proj, expert_gate, expert_up_weight, expert_down, expert_choice, gate_probs,
):
    vm = pl.BlockSpec(memory_space=pltpu.VMEM)
    hbm = pl.BlockSpec(memory_space=pl.ANY)
    V = pltpu.VMEM
    dma = pltpu.SemaphoreType.DMA
    scratch = [
        V((896, D), BF), V((HID, D), BF), V((HID, D), BF),
        V((D, HALF), BF), V((D, HALF), BF), V((HALF, D), BF), V((2, 4, 256, HALF_D), BF),
        V((2, 4, TOK, HALF_D), F32), V((4, PAIR, HALF_D), BF), V((3, PAIR, HALF_D), BF),
        V((2, TOK, HALF_D + 128), F32), V((TOK, HALF_D + 128), F32),
        V((2, 3, 4, 4, 4, PAIR, CARRY), BF),
        V((4, 4, 4, PAIR, HID), F32), V((4, 4, 4, PAIR, HID), F32),
        V((4, SLOTS, CHUNK), BF), V((4 * SLOTS, 128), F32), V((1024, 128), F32),
        V((4, CHUNK, 256), BF), V((4 * SLOTS, D), BF), V((4 * SLOTS, HALF), BF),
    ]
    for _ in range(3):
        scratch += [V((4, 4, 4, PAIR, w), BF) for w in WIDTHS]
    scratch += [V((2, 2, 4, PAIR, w), BF) for w in WIDTHS]
    scratch += [V((2, 4, 4, PAIR, w), BF) for w in WIDTHS]
    scratch += [V((3, 4, PAIR, w), BF) for w in WIDTHS]
    scratch += [V((3, PAIR, w), BF) for w in WIDTHS]
    scratch += [V((2, TOK, HALF_D), F32), V((TOK, HALF_D), F32)]
    scratch += [
        dma((8,)), dma((6,)), dma((3,)), dma((3,)), dma((4,)),
        dma((N_AG,)), dma((N_AG,)), dma((N_RS,)), dma((N_RS,)),
    ]
    both = pl.pallas_call(
        kernel,
        out_shape=jax.ShapeDtypeStruct((2, TOK, D), BF),
        in_specs=[vm, hbm, vm, vm, vm, hbm, hbm, hbm, hbm, hbm, hbm, vm, vm],
        out_specs=vm,
        scratch_shapes=scratch,
        compiler_params=pltpu.CompilerParams(
            collective_id=0, has_side_effects=True, vmem_limit_bytes=63 * 1024 * 1024
        ),
    )(
        attn_heads, out_weight, residual, norm_gain, shared_gate,
        shared_gate_proj.T, shared_up_proj.T, shared_down_proj, expert_gate, expert_up_weight,
        expert_down, expert_choice, gate_probs,
    )
    return both[0], both[1]


def solution(mesh):
    both = ("dp", "tensor")
    in_specs = (
        P("dp", "tensor"), P("tensor", None), P(both, None), P(), P(),
        P(None, both), P(None, both), P(both, None),
        P(both, None, None), P(both, None, None), P(both, None, None),
        P(both, None), P(both, None),
    )
    out_specs = (P(both, None), P(both, None))
    return jax.shard_map(
        on_device, mesh=mesh, in_specs=in_specs, out_specs=out_specs, check_vma=False
    )
```

```python
import jax
import jax.numpy as jnp
from jax import lax
from jax.experimental import pallas as pl
from jax.experimental.pallas import tpu as pltpu
from jax.sharding import PartitionSpec as P

MESH = pl.DeviceIdType.MESH
BF = jnp.bfloat16
F32 = jnp.float32
TOK = 8
PAIR = 16
D = 3584
HALF_D = D // 2
WIDTHS = (640, 640, 512)
OFFS = (0, 640, 1280)
CARRY = 640
ORDERS = ((2, 1, 0), (1, 0, 2), (0, 2, 1))
HID = 160
HALF = 640
EXPERTS = 64
CHUNK = 256
SLOTS = 64
N_AG = 3 * (3 + 3 + 6 + 4)
N_RS = 3 * (6 + 3 + 3)


def silu(v):
    return v / (1.0 + jnp.exp(-v))


def kernel(
    heads, out_w, residual, gain, sgate, sgp, sup, sdn, eg, eu, ed, choice, probs,
    both_out,
    wo, wsg, wsu, weg, weu, wed, rhs,
    part, sbuf, rz, nx, rx, g,
    wd, res, lhs_in, acc_g, acc_u, place, pslot, share_s, lhs, xe, he,
    s0, s1, s2,
    a0, a1, a2, b0, b1, b2, c0, c1, c2, d0, d1, d2,
    fin, rfin,
    w_sem, again_sem, sib_s, sib_r, zs_sem, zr_sem, x_sem, ags, agr, rss, rsr,
):
    dp = lax.axis_index("dp")
    z0 = lax.axis_index("tensor")
    core = lax.rem(dp, 2)
    other = 1 - core
    pos = (dp // 8, lax.rem(dp // 2, 4), z0)

    def device(y, x, c, z):
        return ((y * 4 + x) * 2 + c, z)

    def near(axis, k):
        return lax.rem(pos[axis] + k, 4)

    def peer(axis, k):
        at = list(pos)
        at[axis] = near(axis, k)
        return device(at[0], at[1], core, at[2])

    sibling = device(pos[0], pos[1], other, pos[2])

    wo_load = pltpu.make_async_copy(out_w, wo, w_sem.at[0])
    loads = [
        pltpu.make_async_copy(sgp, wsg, w_sem.at[1]),
        pltpu.make_async_copy(sup, wsu, w_sem.at[2]),
        pltpu.make_async_copy(eg.at[0], weg, w_sem.at[3]),
        pltpu.make_async_copy(eu.at[0], weu, w_sem.at[4]),
        pltpu.make_async_copy(ed.at[0], wed, w_sem.at[5]),
    ]
    for h in range(2):
        cols = pl.ds(h * HALF_D, HALF_D)
        loads.append(pltpu.make_async_copy(sdn.at[:, cols], wd.at[h], w_sem.at[6 + h]))
    wo_load.start()
    for load in loads[0:4]:
        load.start()

    barrier = pltpu.get_barrier_semaphore()
    for axis in range(3):
        for k in range(1, 4):
            pl.semaphore_signal(barrier, inc=1, device_id=peer(axis, k), device_id_type=MESH)
    pl.semaphore_signal(barrier, inc=1, device_id=sibling, device_id_type=MESH)

    def project(j, carry):
        at = pl.multiple_of(j * 256, 256)
        cols = pl.ds(at, 256)
        left = jnp.dot(heads[...], wo[:, cols], preferred_element_type=F32)
        right = jnp.dot(
            heads[...], wo[:, pl.ds(at + HALF_D, 256)], preferred_element_type=F32
        )
        part[0, :, :, cols] = left.reshape(4, TOK, 256)
        part[1, :, :, cols] = right.reshape(4, TOK, 256)
        for q in range(4):
            rows = slice(q * TOK, (q + 1) * TOK)
            sbuf[q, :, cols] = jnp.concatenate([left[rows], right[rows]], axis=0).astype(BF)
        return carry

    wo_load.wait()
    lax.fori_loop(0, 7, project, 0, unroll=True)

    pl.semaphore_wait(barrier, 10)

    zc = []
    for k in range(1, 4):
        c = pltpu.make_async_remote_copy(
            src_ref=sbuf.at[near(2, k)], dst_ref=rz.at[k - 1],
            send_sem=zs_sem.at[k - 1], recv_sem=zr_sem.at[k - 1],
            device_id=peer(2, k), device_id_type=MESH,
        )
        c.start()
        zc.append(c)

    rhs[:, :, HID + SLOTS : 256, :] = jnp.zeros((2, 4, 256 - HID - SLOTS, HALF_D), BF)

    lane = lax.broadcasted_iota(jnp.int32, (TOK, 128), 1)
    facts = jnp.zeros((TOK, 128), F32)
    chosen = choice[...].astype(F32)
    weight = probs[...]
    high = weight.astype(BF).astype(F32)
    low = weight - high
    for k in range(8):
        facts = jnp.where(lane == k, chosen[:, k : k + 1], facts)
        facts = jnp.where(lane == 8 + k, high[:, k : k + 1], facts)
        facts = jnp.where(lane == 16 + k, low[:, k : k + 1], facts)

    for c in zc:
        c.wait_recv()

    square = jnp.zeros((TOK, 1), F32)
    mids = []
    for h in range(2):
        cols = slice(h * HALF_D, (h + 1) * HALF_D)
        total = part[h, z0]
        for k in range(3):
            total = total + rz[k].astype(F32)[h * TOK : (h + 1) * TOK]
        mid = (residual[:, cols].astype(F32) + total).astype(BF)
        both_out[0, :, cols] = mid
        midf = mid.astype(F32)
        mids.append(midf)
        square = square + jnp.sum(midf * midf, axis=1, keepdims=True)
    scale = lax.rsqrt(square * (1.0 / D) + 1e-06)
    logit = jnp.zeros((TOK, 1), F32)
    for h in range(2):
        cols = slice(h * HALF_D, (h + 1) * HALF_D)
        normed = (mids[h] * scale * gain[cols].astype(F32).reshape(1, HALF_D)).astype(BF).astype(F32)
        nx[h, :, 0:HALF_D] = normed
        logit = logit + jnp.sum(normed * sgate[cols].astype(F32).reshape(1, HALF_D), axis=1, keepdims=True)
    share = 1.0 / (1.0 + jnp.exp(-logit))

    share_high = share.astype(BF).astype(F32)
    facts = jnp.where(lane == 24, share_high, facts)
    facts = jnp.where(lane == 25, share - share_high, facts)
    for h in range(2):
        nx[h, :, HALF_D : HALF_D + 128] = facts

    swap = pltpu.make_async_remote_copy(
        src_ref=nx.at[other], dst_ref=rx, send_sem=x_sem.at[0], recv_sem=x_sem.at[1],
        device_id=sibling, device_id_type=MESH,
    )
    swap.start()
    swap.wait_recv()
    mine = nx[core]
    theirs = rx[...]
    first = core == 0
    block = jnp.concatenate(
        [jnp.where(first, mine, theirs), jnp.where(first, theirs, mine)], axis=0
    ).astype(BF)
    for o in range(3):
        g[core, o, pos[0], pos[1], pos[2]] = block[:, o * CARRY : (o + 1) * CARRY]

    again = []
    for y in range(4):
        again.append(
            pltpu.make_async_copy(wd.at[core], rhs.at[0, y, pl.ds(0, HID)], again_sem.at[y])
        )

    def to_sibling(i, src, dst):
        return pltpu.make_async_remote_copy(
            src_ref=src, dst_ref=dst, send_sem=sib_s.at[i], recv_sem=sib_r.at[i],
            device_id=sibling, device_id_type=MESH,
        )

    across = [to_sibling(y, wd.at[other], rhs.at[1, y, pl.ds(0, HID)]) for y in range(4)]

    pending = []
    count = [0]

    def gsend(o, at, dev):
        i = count[0]
        count[0] += 1
        ref = g.at[(core, o) + tuple(at)]
        c = pltpu.make_async_remote_copy(
            src_ref=ref, dst_ref=ref, send_sem=ags.at[i], recv_sem=agr.at[i],
            device_id=dev, device_id_type=MESH,
        )
        c.start()
        pending.append(c)
        return c

    def where_(o, first_, second, third):
        at = [None, None, None]
        for axis, v in zip(ORDERS[o], (first_, second, third)):
            at[axis] = v
        return at

    ALL, A, B = pl.ds(0, 4), pl.ds(0, 2), pl.ds(2, 2)
    own = [[pos[axis] for axis in ORDERS[o]] for o in range(3)]

    got = [[gsend(o, pos, peer(ORDERS[o][0], k)) for k in (1, 3, 2)] for o in range(3)]
    for load in loads[4:]:
        load.start()
    acc_g[...] = jnp.zeros((4, 4, 4, PAIR, HID), F32)
    acc_u[...] = jnp.zeros((4, 4, 4, PAIR, HID), F32)
    for load in loads[0:4]:
        load.wait()

    def absorb(h, o, k):
        at = tuple(where_(o, ALL, ALL, near(ORDERS[o][2], k)))
        x = g[(h, o) + at].reshape(CHUNK, CARRY)[:, : WIDTHS[o]]
        cols = pl.ds(pl.multiple_of(h * HALF_D + OFFS[o], 128), WIDTHS[o])
        turn = (((1,), (1,)), ((), ()))
        for acc, w in ((acc_g, wsg), (acc_u, wsu)):
            r = lax.dot_general(x, w[:, cols], turn, preferred_element_type=F32)
            acc[at] = acc[at] + r.reshape(4, 4, PAIR, HID)

    hop = []
    for o in range(3):
        for c in got[o]:
            c.wait_recv()
        mine_at = where_(o, ALL, own[o][1], own[o][2])
        hop.append([gsend(o, mine_at, peer(ORDERS[o][1], k)) for k in (1, 3, 2)])
    for load in loads[4:]:
        load.wait()
    for copy in again + across:
        copy.start()
    stage = []
    sib = [[], [], []]
    for o in range(3):
        for c in hop[o]:
            c.wait_recv()
        ax = ORDERS[o][2]
        at_a = where_(o, A, ALL, own[o][2])
        at_b = where_(o, B, ALL, own[o][2])
        ra = gsend(o, at_a, peer(ax, 1))
        lb = gsend(o, at_b, peer(ax, 3))
        rb = gsend(o, at_b, peer(ax, 1))
        la = gsend(o, at_a, peer(ax, 3))
        stage.append((ra, lb, rb, la))
        sib[o].append(gsend(o, where_(o, ALL, ALL, own[o][2]), sibling))
    for o in range(3):
        absorb(core, o, 0)
    for o in range(3):
        sib[o][0].wait_recv()
        absorb(other, o, 0)
    hop = [[], [], []]
    for event in range(4):
        for o in range(3):
            ax = ORDERS[o][2]
            half = (A, B, B, A)[event]
            came = near(ax, (3, 1, 3, 1)[event])
            at = where_(o, half, ALL, came)
            stage[o][event].wait_recv()
            if event < 2:
                hop[o].append(gsend(o, at, peer(ax, (1, 3)[event])))
            if event >= 2:
                sib[o].append(gsend(o, where_(o, ALL, ALL, came), sibling))
    for o in range(3):
        absorb(core, o, 3)
        absorb(core, o, 1)
    for o in range(3):
        sib[o][1].wait_recv()
        absorb(other, o, 3)
        sib[o][2].wait_recv()
        absorb(other, o, 1)
    for o in range(3):
        for c in hop[o]:
            c.wait_recv()
        sib[o].append(gsend(o, where_(o, ALL, ALL, near(ORDERS[o][2], 2)), sibling))

    expert = lax.rem(dp * 4 + z0, EXPERTS).astype(F32)
    told = g[core, 2, :, :, :, :, 512:640].reshape(1024, 128).astype(F32)
    share_s[...] = jnp.broadcast_to(told[:, 24:25] + told[:, 25:26], (1024, 128))
    turned = told.T
    hit8 = turned[0:8] == expert
    p_row = jnp.sum(jnp.where(hit8, turned[8:16] + turned[16:24], 0.0), axis=0, keepdims=True)
    hit = jnp.sum(jnp.where(hit8, 1.0, 0.0), axis=0, keepdims=True)
    hit = jnp.broadcast_to(hit, (8, 1024))
    token = lax.broadcasted_iota(jnp.int32, (8, 1024), 1)
    rank = jnp.zeros((8, 1024), F32)
    for k in range(1, 8):
        rank = rank + jnp.where(lax.rem(token, 8) >= k, pltpu.roll(hit, k, axis=1), 0.0)
    row = (lax.rem(token // 8, 32) * 2).astype(F32) + rank
    row = jnp.where(hit > 0.5, row, -1000.0)
    row1 = row[0:1]
    column = jnp.broadcast_to(row1, (128, 1024)).T
    lane1 = lax.broadcasted_iota(jnp.int32, (1024, 128), 1).astype(F32)
    lhs[:, :, 0:128] = jnp.zeros((4, CHUNK, 128), BF)
    lhs[:, :, 128:256] = (
        jnp.where(lane1 - (HID - 128.0) == column, 1.0, 0.0).astype(BF).reshape(4, CHUNK, 128)
    )
    slot_id = lax.broadcasted_iota(jnp.int32, (SLOTS, CHUNK), 0).astype(F32)
    for y in range(4):
        cols = slice(y * CHUNK, (y + 1) * CHUNK)
        chosen_y = jnp.where(slot_id == row1[:, cols], 1.0, 0.0)
        place[y] = chosen_y.astype(BF)
        pslot[pl.ds(y * SLOTS, SLOTS)] = jnp.broadcast_to(
            jnp.sum(chosen_y * p_row[:, cols], axis=1, keepdims=True), (SLOTS, 128)
        )

    def pick(h):
        for y in range(4):
            for o in range(3):
                x = g[h, o, y].reshape(CHUNK, CARRY)[:, : WIDTHS[o]]
                r = jnp.dot(place[y], x, preferred_element_type=F32)
                xe[h, y * SLOTS : (y + 1) * SLOTS, OFFS[o] : OFFS[o] + WIDTHS[o]] = r.astype(BF)

    for o in range(3):
        absorb(core, o, 2)
    pick(core)
    for o in range(3):
        sib[o][3].wait_recv()
        absorb(other, o, 2)
    pick(other)
    for y in range(4):
        share_y = share_s[y * CHUNK : (y + 1) * CHUNK]
        hs = silu(acc_g[y].reshape(CHUNK, HID)) * acc_u[y].reshape(CHUNK, HID)
        lhs[y, :, 0:128] = (hs[:, 0:128] * share_y).astype(BF)
        lhs[y, :, 128:HID] = (hs[:, 128:HID] * share_y[:, 0 : HID - 128]).astype(BF)

    lhs_over = to_sibling(4, lhs, lhs_in)
    lhs_over.start()

    def expert_hidden(i, carry):
        cols = pl.ds(pl.multiple_of(i * 128, 128), 128)
        w = jnp.concatenate([weg[:, cols], weu[:, cols]], axis=1)
        rows = jnp.concatenate([xe[0], xe[1]], axis=1)
        r = jnp.dot(rows, w, preferred_element_type=F32)
        he[:, cols] = (silu(r[:, 0:128]) * r[:, 128:256]).astype(BF)
        return carry

    lax.fori_loop(0, HALF // 128, expert_hidden, 0, unroll=True)

    def expert_down(h, at, w):
        cols = pl.ds(pl.multiple_of(h * HALF_D + at, 128), w)
        r = jnp.dot(he[...], wed[:, cols], preferred_element_type=F32)
        return (r * jnp.concatenate([pslot[...]] * (w // 128), axis=1)).astype(BF)

    res_over = []
    for o in range(3):
        cols = slice(OFFS[o], OFFS[o] + WIDTHS[o])
        down = expert_down(other, OFFS[o], WIDTHS[o])
        res[:, :, cols] = down.reshape(4, SLOTS, WIDTHS[o])
        cols = pl.ds(OFFS[o], WIDTHS[o])
        over = to_sibling(5 + o, res.at[:, :, cols], rhs.at[1, :, pl.ds(HID, SLOTS), cols])
        over.start()
        res_over.append(over)
    for o in range(3):
        cols = slice(OFFS[o], OFFS[o] + WIDTHS[o])
        down = expert_down(core, OFFS[o], WIDTHS[o])
        rhs[0, :, HID : HID + SLOTS, cols] = down.reshape(4, SLOTS, WIDTHS[o])
    for copy in again:
        copy.wait()
    for c in across + [lhs_over]:
        c.wait_recv()

    s = (s0, s1, s2)
    n_gather = len(pending)
    half_in = (a0, a1, a2)
    full_in = (b0, b1, b2)
    last_in = (c0, c1, c2)
    one_in = (d0, d1, d2)
    count[0] = 0

    def rsend(src, dst, dev):
        i = count[0]
        count[0] += 1
        c = pltpu.make_async_remote_copy(
            src_ref=src, dst_ref=dst, send_sem=rss.at[i], recv_sem=rsr.at[i],
            device_id=dev, device_id_type=MESH,
        )
        c.start()
        pending.append(c)
        return c

    def combine(o):
        cols = slice(OFFS[o], OFFS[o] + WIDTHS[o])
        for y in range(4):
            r = jnp.dot(lhs[y], rhs[0, y, :, cols], preferred_element_type=F32)
            r = r + jnp.dot(lhs_in[y], rhs[1, y, :, cols], preferred_element_type=F32)
            s[o][y] = r.astype(BF).reshape(4, 4, PAIR, WIDTHS[o])

    def at1(o, c, half):
        rest = [half, ALL]
        return tuple(c if axis == ORDERS[o][2] else rest.pop(0) for axis in range(3))

    def add1(o, c, lo, hi, terms):
        def step(i, carry):
            at = at1(o, c, i)
            total = s[o][at].astype(F32)
            for term, base in terms:
                total = total + term[i - base].astype(F32)
            s[o][at] = total.astype(BF)
            return carry

        lax.fori_loop(lo, hi, step, 0)

    stage = [[], [], []]
    for o in range(3):
        res_over[o].wait_recv()
        combine(o)
        ax = ORDERS[o][2]
        far = near(ax, 2)
        stage[o] += [
            rsend(s[o].at[at1(o, far, A)], half_in[o].at[0], peer(ax, 1)),
            rsend(s[o].at[at1(o, far, B)], half_in[o].at[1], peer(ax, 3)),
            rsend(s[o].at[at1(o, near(ax, 1), B)], full_in[o].at[0, B], peer(ax, 1)),
            rsend(s[o].at[at1(o, near(ax, 3), A)], full_in[o].at[1, A], peer(ax, 3)),
        ]
    for c in zc + [swap] + across + [lhs_over] + res_over + pending[:n_gather]:
        c.wait_send()
    for o in range(3):
        ax = ORDERS[o][2]
        c = near(ax, 1)
        stage[o][0].wait_recv()
        add1(o, c, 0, 2, [(half_in[o].at[0], 0)])
        stage[o].append(rsend(s[o].at[at1(o, c, A)], full_in[o].at[0, A], peer(ax, 1)))
        c = near(ax, 3)
        stage[o][1].wait_recv()
        add1(o, c, 2, 4, [(half_in[o].at[1], 2)])
        stage[o].append(rsend(s[o].at[at1(o, c, B)], full_in[o].at[1, B], peer(ax, 3)))

    def at2(o, c):
        return tuple(where_(o, ALL, c, own[o][2]))

    stage2 = []
    for o in range(3):
        for c in stage[o][2:]:
            c.wait_recv()
        add1(o, own[o][2], 0, 4, [(full_in[o].at[0], 0), (full_in[o].at[1], 0)])
        ax = ORDERS[o][1]
        stage2.append(
            [
                rsend(s[o].at[at2(o, near(ax, k))], last_in[o].at[k - 1], peer(ax, k))
                for k in (1, 3, 2)
            ]
        )

    for c in pending[n_gather : n_gather + 18]:
        c.wait_send()
    stage3 = []
    for o in range(3):
        for c in stage2[o]:
            c.wait_recv()
        at = at2(o, own[o][1])
        total = s[o][at].astype(F32)
        for k in range(3):
            total = total + last_in[o][k].astype(F32)
        s[o][at] = total.astype(BF)
        ax = ORDERS[o][0]
        stage3.append(
            [
                rsend(
                    s[o].at[tuple(where_(o, near(ax, k), own[o][1], own[o][2]))],
                    one_in[o].at[k - 1],
                    peer(ax, k),
                )
                for k in (1, 2, 3)
            ]
        )
    for o in range(3):
        total = s[o][pos].astype(F32)
        for k in range(3):
            stage3[o][k].wait_recv()
            total = total + one_in[o][k].astype(F32)
        cols = pl.ds(OFFS[o], WIDTHS[o])
        fin[0, :, cols] = total[0:TOK]
        fin[1, :, cols] = total[TOK:PAIR]

    swap_back = pltpu.make_async_remote_copy(
        src_ref=fin.at[other], dst_ref=rfin, send_sem=x_sem.at[2], recv_sem=x_sem.at[3],
        device_id=sibling, device_id_type=MESH,
    )
    swap_back.start()
    swap_back.wait_recv()
    mine = fin[core]
    theirs = rfin[...]
    both_out[1, :, 0:HALF_D] = jnp.where(first, mine, theirs).astype(BF)
    both_out[1, :, HALF_D:D] = jnp.where(first, theirs, mine).astype(BF)

    swap_back.wait_send()
    for c in pending[n_gather + 18 :]:
        c.wait_send()


def on_device(
    attn_heads, out_weight, residual, norm_gain, shared_gate, shared_gate_proj, shared_up_proj,
    shared_down_proj, expert_gate, expert_up_weight, expert_down, expert_choice, gate_probs,
):
    vm = pl.BlockSpec(memory_space=pltpu.VMEM)
    hbm = pl.BlockSpec(memory_space=pl.ANY)
    V = pltpu.VMEM
    dma = pltpu.SemaphoreType.DMA
    scratch = [
        V((896, D), BF), V((HID, D), BF), V((HID, D), BF),
        V((D, HALF), BF), V((D, HALF), BF), V((HALF, D), BF), V((2, 4, 256, HALF_D), BF),
        V((2, 4, TOK, HALF_D), F32), V((4, PAIR, HALF_D), BF), V((3, PAIR, HALF_D), BF),
        V((2, TOK, HALF_D + 128), F32), V((TOK, HALF_D + 128), F32),
        V((2, 3, 4, 4, 4, PAIR, CARRY), BF),
        V((2, HID, HALF_D), BF), V((4, SLOTS, HALF_D), BF), V((4, CHUNK, 256), BF),
        V((4, 4, 4, PAIR, HID), F32), V((4, 4, 4, PAIR, HID), F32),
        V((4, SLOTS, CHUNK), BF), V((4 * SLOTS, 128), F32), V((1024, 128), F32),
        V((4, CHUNK, 256), BF), V((2, 4 * SLOTS, HALF_D), BF), V((4 * SLOTS, HALF), BF),
    ]
    scratch += [V((4, 4, 4, PAIR, w), BF) for w in WIDTHS]
    scratch += [V((2, 2, 4, PAIR, w), BF) for w in WIDTHS]
    scratch += [V((2, 4, 4, PAIR, w), BF) for w in WIDTHS]
    scratch += [V((3, 4, PAIR, w), BF) for w in WIDTHS]
    scratch += [V((3, PAIR, w), BF) for w in WIDTHS]
    scratch += [V((2, TOK, HALF_D), F32), V((TOK, HALF_D), F32)]
    scratch += [
        dma((8,)), dma((4,)), dma((8,)), dma((8,)), dma((3,)), dma((3,)), dma((4,)),
        dma((N_AG,)), dma((N_AG,)), dma((N_RS,)), dma((N_RS,)),
    ]
    both = pl.pallas_call(
        kernel,
        out_shape=jax.ShapeDtypeStruct((2, TOK, D), BF),
        in_specs=[vm, hbm, vm, vm, vm, hbm, hbm, hbm, hbm, hbm, hbm, vm, vm],
        out_specs=vm,
        scratch_shapes=scratch,
        compiler_params=pltpu.CompilerParams(
            collective_id=0, has_side_effects=True, vmem_limit_bytes=63 * 1024 * 1024
        ),
    )(
        attn_heads, out_weight, residual, norm_gain, shared_gate,
        shared_gate_proj.T, shared_up_proj.T, shared_down_proj, expert_gate, expert_up_weight,
        expert_down, expert_choice, gate_probs,
    )
    return both[0], both[1]


def solution(mesh):
    both = ("dp", "tensor")
    in_specs = (
        P("dp", "tensor"), P("tensor", None), P(both, None), P(), P(),
        P(None, both), P(None, both), P(both, None),
        P(both, None, None), P(both, None, None), P(both, None, None),
        P(both, None), P(both, None),
    )
    out_specs = (P(both, None), P(both, None))
    return jax.shard_map(
        on_device, mesh=mesh, in_specs=in_specs, out_specs=out_specs, check_vma=False
    )
```

```python
import jax
import jax.numpy as jnp
from jax import lax
from jax.experimental import pallas as pl
from jax.experimental.pallas import tpu as pltpu
from jax.sharding import PartitionSpec as P

MESH = pl.DeviceIdType.MESH
BF = jnp.bfloat16
F32 = jnp.float32
TOK = 8
PAIR = 16
D = 3584
HALF_D = D // 2
WIDTHS = (640, 640, 512)
OFFS = (0, 640, 1280)
CARRY = 640
ORDERS = ((2, 1, 0), (1, 0, 2), (0, 2, 1))
HID = 160
HALF = 640
EXPERTS = 64
CHUNK = 256
SLOTS = 64
N_AG = 3 * (3 + 3 + 6 + 4)
N_RS = 3 * (6 + 3 + 3)


def silu(v):
    return v / (1.0 + jnp.exp(-v))


def kernel(
    heads, out_w, residual, gain, sgate, sgp, sup, sdn, eg, eu, ed, choice, probs,
    both_out,
    wo, wsg, wsu, weg, weu, wed, rhs,
    part, sbuf, rz, nx, rx, g,
    wd, res, lhs_in, acc_g, acc_u, place, pslot, share_s, lhs, xe, he,
    s0, s1, s2,
    a0, a1, a2, b0, b1, b2, c0, c1, c2, d0, d1, d2,
    fin, rfin,
    w_sem, again_sem, sib_s, sib_r, zs_sem, zr_sem, x_sem, ags, agr, rss, rsr,
):
    dp = lax.axis_index("dp")
    z0 = lax.axis_index("tensor")
    core = lax.rem(dp, 2)
    other = 1 - core
    pos = (dp // 8, lax.rem(dp // 2, 4), z0)

    def device(y, x, c, z):
        return ((y * 4 + x) * 2 + c, z)

    def near(axis, k):
        return lax.rem(pos[axis] + k, 4)

    def peer(axis, k):
        at = list(pos)
        at[axis] = near(axis, k)
        return device(at[0], at[1], core, at[2])

    sibling = device(pos[0], pos[1], other, pos[2])

    wo_load = pltpu.make_async_copy(out_w, wo, w_sem.at[0])
    loads = [
        pltpu.make_async_copy(sgp, wsg, w_sem.at[1]),
        pltpu.make_async_copy(sup, wsu, w_sem.at[2]),
        pltpu.make_async_copy(eg.at[0], weg, w_sem.at[3]),
        pltpu.make_async_copy(eu.at[0], weu, w_sem.at[4]),
        pltpu.make_async_copy(ed.at[0], wed, w_sem.at[5]),
    ]
    for h in range(2):
        cols = pl.ds(h * HALF_D, HALF_D)
        loads.append(pltpu.make_async_copy(sdn.at[:, cols], wd.at[h], w_sem.at[6 + h]))
    wo_load.start()
    for load in loads[0:4]:
        load.start()

    barrier = pltpu.get_barrier_semaphore()
    for axis in range(3):
        for k in range(1, 4):
            pl.semaphore_signal(barrier, inc=1, device_id=peer(axis, k), device_id_type=MESH)
    pl.semaphore_signal(barrier, inc=1, device_id=sibling, device_id_type=MESH)

    def project(j, carry):
        at = pl.multiple_of(j * 256, 256)
        cols = pl.ds(at, 256)
        left = jnp.dot(heads[...], wo[:, cols], preferred_element_type=F32)
        right = jnp.dot(
            heads[...], wo[:, pl.ds(at + HALF_D, 256)], preferred_element_type=F32
        )
        part[0, :, :, cols] = left.reshape(4, TOK, 256)
        part[1, :, :, cols] = right.reshape(4, TOK, 256)
        for q in range(4):
            rows = slice(q * TOK, (q + 1) * TOK)
            sbuf[q, :, cols] = jnp.concatenate([left[rows], right[rows]], axis=0).astype(BF)
        return carry

    wo_load.wait()
    lax.fori_loop(0, 7, project, 0, unroll=True)

    pl.semaphore_wait(barrier, 10)

    zc = []
    for k in (2, 1, 3):
        c = pltpu.make_async_remote_copy(
            src_ref=sbuf.at[near(2, k)], dst_ref=rz.at[k - 1],
            send_sem=zs_sem.at[k - 1], recv_sem=zr_sem.at[k - 1],
            device_id=peer(2, k), device_id_type=MESH,
        )
        c.start()
        zc.append(c)

    rhs[:, :, HID + SLOTS : 256, :] = jnp.zeros((2, 4, 256 - HID - SLOTS, HALF_D), BF)

    lane = lax.broadcasted_iota(jnp.int32, (TOK, 128), 1)
    facts = jnp.zeros((TOK, 128), F32)
    chosen = choice[...].astype(F32)
    weight = probs[...]
    high = weight.astype(BF).astype(F32)
    low = weight - high
    for k in range(8):
        facts = jnp.where(lane == k, chosen[:, k : k + 1], facts)
        facts = jnp.where(lane == 8 + k, high[:, k : k + 1], facts)
        facts = jnp.where(lane == 16 + k, low[:, k : k + 1], facts)

    for c in zc:
        c.wait_recv()

    square = jnp.zeros((TOK, 1), F32)
    mids = []
    for h in range(2):
        cols = slice(h * HALF_D, (h + 1) * HALF_D)
        total = part[h, z0]
        for k in range(3):
            total = total + rz[k].astype(F32)[h * TOK : (h + 1) * TOK]
        mid = (residual[:, cols].astype(F32) + total).astype(BF)
        both_out[0, :, cols] = mid
        midf = mid.astype(F32)
        mids.append(midf)
        square = square + jnp.sum(midf * midf, axis=1, keepdims=True)
    scale = lax.rsqrt(square * (1.0 / D) + 1e-06)
    logit = jnp.zeros((TOK, 1), F32)
    for h in range(2):
        cols = slice(h * HALF_D, (h + 1) * HALF_D)
        normed = (mids[h] * scale * gain[cols].astype(F32).reshape(1, HALF_D)).astype(BF).astype(F32)
        nx[h, :, 0:HALF_D] = normed
        logit = logit + jnp.sum(normed * sgate[cols].astype(F32).reshape(1, HALF_D), axis=1, keepdims=True)
    share = 1.0 / (1.0 + jnp.exp(-logit))

    share_high = share.astype(BF).astype(F32)
    facts = jnp.where(lane == 24, share_high, facts)
    facts = jnp.where(lane == 25, share - share_high, facts)
    for h in range(2):
        nx[h, :, HALF_D : HALF_D + 128] = facts

    swap = pltpu.make_async_remote_copy(
        src_ref=nx.at[other], dst_ref=rx, send_sem=x_sem.at[0], recv_sem=x_sem.at[1],
        device_id=sibling, device_id_type=MESH,
    )
    swap.start()
    swap.wait_recv()
    mine = nx[core]
    theirs = rx[...]
    first = core == 0
    block = jnp.concatenate(
        [jnp.where(first, mine, theirs), jnp.where(first, theirs, mine)], axis=0
    ).astype(BF)
    for o in range(3):
        g[core, o, pos[0], pos[1], pos[2]] = block[:, o * CARRY : (o + 1) * CARRY]

    again = []
    for y in range(4):
        again.append(
            pltpu.make_async_copy(wd.at[core], rhs.at[0, y, pl.ds(0, HID)], again_sem.at[y])
        )

    def to_sibling(i, src, dst):
        return pltpu.make_async_remote_copy(
            src_ref=src, dst_ref=dst, send_sem=sib_s.at[i], recv_sem=sib_r.at[i],
            device_id=sibling, device_id_type=MESH,
        )

    across = [to_sibling(y, wd.at[other], rhs.at[1, y, pl.ds(0, HID)]) for y in range(4)]

    pending = []
    count = [0]

    def gsend(o, at, dev):
        i = count[0]
        count[0] += 1
        ref = g.at[(core, o) + tuple(at)]
        c = pltpu.make_async_remote_copy(
            src_ref=ref, dst_ref=ref, send_sem=ags.at[i], recv_sem=agr.at[i],
            device_id=dev, device_id_type=MESH,
        )
        c.start()
        pending.append(c)
        return c

    def where_(o, first_, second, third):
        at = [None, None, None]
        for axis, v in zip(ORDERS[o], (first_, second, third)):
            at[axis] = v
        return at

    ALL, A, B = pl.ds(0, 4), pl.ds(0, 2), pl.ds(2, 2)
    own = [[pos[axis] for axis in ORDERS[o]] for o in range(3)]

    got = [[gsend(o, pos, peer(ORDERS[o][0], k)) for k in (2, 1, 3)] for o in range(3)]
    for load in loads[4:]:
        load.start()
    acc_g[...] = jnp.zeros((4, 4, 4, PAIR, HID), F32)
    acc_u[...] = jnp.zeros((4, 4, 4, PAIR, HID), F32)
    for load in loads[0:4]:
        load.wait()

    def absorb(h, o, k):
        at = tuple(where_(o, ALL, ALL, near(ORDERS[o][2], k)))
        x = g[(h, o) + at].reshape(CHUNK, CARRY)[:, : WIDTHS[o]]
        cols = pl.ds(pl.multiple_of(h * HALF_D + OFFS[o], 128), WIDTHS[o])
        turn = (((1,), (1,)), ((), ()))
        for acc, w in ((acc_g, wsg), (acc_u, wsu)):
            r = lax.dot_general(x, w[:, cols], turn, preferred_element_type=F32)
            acc[at] = acc[at] + r.reshape(4, 4, PAIR, HID)

    hop = []
    for o in range(3):
        for c in got[o]:
            c.wait_recv()
        mine_at = where_(o, ALL, own[o][1], own[o][2])
        hop.append([gsend(o, mine_at, peer(ORDERS[o][1], k)) for k in (2, 1, 3)])
    for load in loads[4:]:
        load.wait()
    for copy in again + across:
        copy.start()
    stage = []
    sib = [[], [], []]
    for o in range(3):
        for c in hop[o]:
            c.wait_recv()
        ax = ORDERS[o][2]
        at_a = where_(o, A, ALL, own[o][2])
        at_b = where_(o, B, ALL, own[o][2])
        ra = gsend(o, at_a, peer(ax, 1))
        lb = gsend(o, at_b, peer(ax, 3))
        rb = gsend(o, at_b, peer(ax, 1))
        la = gsend(o, at_a, peer(ax, 3))
        stage.append((ra, lb, rb, la))
        sib[o].append(gsend(o, where_(o, ALL, ALL, own[o][2]), sibling))
    for o in range(3):
        absorb(core, o, 0)
    for o in range(3):
        sib[o][0].wait_recv()
        absorb(other, o, 0)
    hop = [[], [], []]
    for event in range(4):
        for o in range(3):
            ax = ORDERS[o][2]
            half = (A, B, B, A)[event]
            came = near(ax, (3, 1, 3, 1)[event])
            at = where_(o, half, ALL, came)
            stage[o][event].wait_recv()
            if event < 2:
                hop[o].append(gsend(o, at, peer(ax, (1, 3)[event])))
            if event >= 2:
                sib[o].append(gsend(o, where_(o, ALL, ALL, came), sibling))
    for o in range(3):
        absorb(core, o, 3)
        absorb(core, o, 1)
    for o in range(3):
        sib[o][1].wait_recv()
        absorb(other, o, 3)
        sib[o][2].wait_recv()
        absorb(other, o, 1)
    for o in range(3):
        for c in hop[o]:
            c.wait_recv()
        sib[o].append(gsend(o, where_(o, ALL, ALL, near(ORDERS[o][2], 2)), sibling))

    expert = lax.rem(dp * 4 + z0, EXPERTS).astype(F32)
    told = g[core, 2, :, :, :, :, 512:640].reshape(1024, 128).astype(F32)
    share_s[...] = jnp.broadcast_to(told[:, 24:25] + told[:, 25:26], (1024, 128))
    turned = told.T
    hit8 = turned[0:8] == expert
    p_row = jnp.sum(jnp.where(hit8, turned[8:16] + turned[16:24], 0.0), axis=0, keepdims=True)
    hit = jnp.sum(jnp.where(hit8, 1.0, 0.0), axis=0, keepdims=True)
    hit = jnp.broadcast_to(hit, (8, 1024))
    token = lax.broadcasted_iota(jnp.int32, (8, 1024), 1)
    rank = jnp.zeros((8, 1024), F32)
    for k in range(1, 8):
        rank = rank + jnp.where(lax.rem(token, 8) >= k, pltpu.roll(hit, k, axis=1), 0.0)
    row = (lax.rem(token // 8, 32) * 2).astype(F32) + rank
    row = jnp.where(hit > 0.5, row, -1000.0)
    row1 = row[0:1]
    column = jnp.broadcast_to(row1, (128, 1024)).T
    lane1 = lax.broadcasted_iota(jnp.int32, (1024, 128), 1).astype(F32)
    lhs[:, :, 0:128] = jnp.zeros((4, CHUNK, 128), BF)
    lhs[:, :, 128:256] = (
        jnp.where(lane1 - (HID - 128.0) == column, 1.0, 0.0).astype(BF).reshape(4, CHUNK, 128)
    )
    slot_id = lax.broadcasted_iota(jnp.int32, (SLOTS, CHUNK), 0).astype(F32)
    for y in range(4):
        cols = slice(y * CHUNK, (y + 1) * CHUNK)
        chosen_y = jnp.where(slot_id == row1[:, cols], 1.0, 0.0)
        place[y] = chosen_y.astype(BF)
        pslot[pl.ds(y * SLOTS, SLOTS)] = jnp.broadcast_to(
            jnp.sum(chosen_y * p_row[:, cols], axis=1, keepdims=True), (SLOTS, 128)
        )

    def pick(h):
        for y in range(4):
            for o in range(3):
                x = g[h, o, y].reshape(CHUNK, CARRY)[:, : WIDTHS[o]]
                r = jnp.dot(place[y], x, preferred_element_type=F32)
                xe[h, y * SLOTS : (y + 1) * SLOTS, OFFS[o] : OFFS[o] + WIDTHS[o]] = r.astype(BF)

    for o in range(3):
        absorb(core, o, 2)
    pick(core)
    for o in range(3):
        sib[o][3].wait_recv()
        absorb(other, o, 2)
    pick(other)
    for y in range(4):
        share_y = share_s[y * CHUNK : (y + 1) * CHUNK]
        hs = silu(acc_g[y].reshape(CHUNK, HID)) * acc_u[y].reshape(CHUNK, HID)
        lhs[y, :, 0:128] = (hs[:, 0:128] * share_y).astype(BF)
        lhs[y, :, 128:HID] = (hs[:, 128:HID] * share_y[:, 0 : HID - 128]).astype(BF)

    lhs_over = to_sibling(4, lhs, lhs_in)
    lhs_over.start()

    def expert_hidden(i, carry):
        cols = pl.ds(pl.multiple_of(i * 128, 128), 128)
        w = jnp.concatenate([weg[:, cols], weu[:, cols]], axis=1)
        rows = jnp.concatenate([xe[0], xe[1]], axis=1)
        r = jnp.dot(rows, w, preferred_element_type=F32)
        he[:, cols] = (silu(r[:, 0:128]) * r[:, 128:256]).astype(BF)
        return carry

    lax.fori_loop(0, HALF // 128, expert_hidden, 0, unroll=True)

    def expert_down(h, at, w):
        cols = pl.ds(pl.multiple_of(h * HALF_D + at, 128), w)
        r = jnp.dot(he[...], wed[:, cols], preferred_element_type=F32)
        return (r * jnp.concatenate([pslot[...]] * (w // 128), axis=1)).astype(BF)

    res_over = []
    for o in range(3):
        cols = slice(OFFS[o], OFFS[o] + WIDTHS[o])
        down = expert_down(other, OFFS[o], WIDTHS[o])
        res[:, :, cols] = down.reshape(4, SLOTS, WIDTHS[o])
        cols = pl.ds(OFFS[o], WIDTHS[o])
        over = to_sibling(5 + o, res.at[:, :, cols], rhs.at[1, :, pl.ds(HID, SLOTS), cols])
        over.start()
        res_over.append(over)
    for o in range(3):
        cols = slice(OFFS[o], OFFS[o] + WIDTHS[o])
        down = expert_down(core, OFFS[o], WIDTHS[o])
        rhs[0, :, HID : HID + SLOTS, cols] = down.reshape(4, SLOTS, WIDTHS[o])
    for copy in again:
        copy.wait()
    for c in across + [lhs_over]:
        c.wait_recv()

    s = (s0, s1, s2)
    n_gather = len(pending)
    half_in = (a0, a1, a2)
    full_in = (b0, b1, b2)
    last_in = (c0, c1, c2)
    one_in = (d0, d1, d2)
    count[0] = 0

    def rsend(src, dst, dev):
        i = count[0]
        count[0] += 1
        c = pltpu.make_async_remote_copy(
            src_ref=src, dst_ref=dst, send_sem=rss.at[i], recv_sem=rsr.at[i],
            device_id=dev, device_id_type=MESH,
        )
        c.start()
        pending.append(c)
        return c

    def combine(o):
        cols = slice(OFFS[o], OFFS[o] + WIDTHS[o])
        for y in range(4):
            r = jnp.dot(lhs[y], rhs[0, y, :, cols], preferred_element_type=F32)
            r = r + jnp.dot(lhs_in[y], rhs[1, y, :, cols], preferred_element_type=F32)
            s[o][y] = r.astype(BF).reshape(4, 4, PAIR, WIDTHS[o])

    def at1(o, c, half):
        rest = [half, ALL]
        return tuple(c if axis == ORDERS[o][2] else rest.pop(0) for axis in range(3))

    def add1(o, c, lo, hi, terms):
        def step(i, carry):
            at = at1(o, c, i)
            total = s[o][at].astype(F32)
            for term, base in terms:
                total = total + term[i - base].astype(F32)
            s[o][at] = total.astype(BF)
            return carry

        lax.fori_loop(lo, hi, step, 0)

    stage = [[], [], []]
    for o in range(3):
        res_over[o].wait_recv()
        combine(o)
        ax = ORDERS[o][2]
        far = near(ax, 2)
        stage[o] += [
            rsend(s[o].at[at1(o, far, A)], half_in[o].at[0], peer(ax, 1)),
            rsend(s[o].at[at1(o, far, B)], half_in[o].at[1], peer(ax, 3)),
            rsend(s[o].at[at1(o, near(ax, 1), B)], full_in[o].at[0, B], peer(ax, 1)),
            rsend(s[o].at[at1(o, near(ax, 3), A)], full_in[o].at[1, A], peer(ax, 3)),
        ]
    for c in zc + [swap] + across + [lhs_over] + res_over + pending[:n_gather]:
        c.wait_send()
    for o in range(3):
        ax = ORDERS[o][2]
        c = near(ax, 1)
        stage[o][0].wait_recv()
        add1(o, c, 0, 2, [(half_in[o].at[0], 0)])
        stage[o].append(rsend(s[o].at[at1(o, c, A)], full_in[o].at[0, A], peer(ax, 1)))
        c = near(ax, 3)
        stage[o][1].wait_recv()
        add1(o, c, 2, 4, [(half_in[o].at[1], 2)])
        stage[o].append(rsend(s[o].at[at1(o, c, B)], full_in[o].at[1, B], peer(ax, 3)))

    def at2(o, c):
        return tuple(where_(o, ALL, c, own[o][2]))

    def line_sum(o, c):
        rest = [axis for axis in range(3) if axis != ORDERS[o][2]]
        at = (c,) if rest[0] == ORDERS[o][1] else (ALL, c)
        total = s[o][at2(o, c)].astype(F32)
        for side in range(2):
            total = total + full_in[o][(side,) + at].astype(F32)
        return total

    stage2 = []
    for o in range(3):
        for c in stage[o][2:]:
            c.wait_recv()
        ax = ORDERS[o][1]
        sent = []
        for k in (2, 1, 3):
            at = at2(o, near(ax, k))
            s[o][at] = line_sum(o, near(ax, k)).astype(BF)
            sent.append(rsend(s[o].at[at], last_in[o].at[k - 1], peer(ax, k)))
        stage2.append(sent)

    for c in pending[n_gather : n_gather + 18]:
        c.wait_send()
    stage3 = []
    for o in range(3):
        for c in stage2[o]:
            c.wait_recv()
        at = at2(o, own[o][1])
        total = line_sum(o, own[o][1])
        for k in range(3):
            total = total + last_in[o][k].astype(F32)
        s[o][at] = total.astype(BF)
        ax = ORDERS[o][0]
        stage3.append(
            [
                rsend(
                    s[o].at[tuple(where_(o, near(ax, k), own[o][1], own[o][2]))],
                    one_in[o].at[k - 1],
                    peer(ax, k),
                )
                for k in (2, 1, 3)
            ]
        )
    for o in range(3):
        total = s[o][pos].astype(F32)
        for c in stage3[o]:
            c.wait_recv()
        for k in range(3):
            total = total + one_in[o][k].astype(F32)
        cols = pl.ds(OFFS[o], WIDTHS[o])
        fin[0, :, cols] = total[0:TOK]
        fin[1, :, cols] = total[TOK:PAIR]

    swap_back = pltpu.make_async_remote_copy(
        src_ref=fin.at[other], dst_ref=rfin, send_sem=x_sem.at[2], recv_sem=x_sem.at[3],
        device_id=sibling, device_id_type=MESH,
    )
    swap_back.start()
    swap_back.wait_recv()
    mine = fin[core]
    theirs = rfin[...]
    both_out[1, :, 0:HALF_D] = jnp.where(first, mine, theirs).astype(BF)
    both_out[1, :, HALF_D:D] = jnp.where(first, theirs, mine).astype(BF)

    swap_back.wait_send()
    for c in pending[n_gather + 18 :]:
        c.wait_send()


def on_device(
    attn_heads, out_weight, residual, norm_gain, shared_gate, shared_gate_proj, shared_up_proj,
    shared_down_proj, expert_gate, expert_up_weight, expert_down, expert_choice, gate_probs,
):
    vm = pl.BlockSpec(memory_space=pltpu.VMEM)
    hbm = pl.BlockSpec(memory_space=pl.ANY)
    V = pltpu.VMEM
    dma = pltpu.SemaphoreType.DMA
    scratch = [
        V((896, D), BF), V((HID, D), BF), V((HID, D), BF),
        V((D, HALF), BF), V((D, HALF), BF), V((HALF, D), BF), V((2, 4, 256, HALF_D), BF),
        V((2, 4, TOK, HALF_D), F32), V((4, PAIR, HALF_D), BF), V((3, PAIR, HALF_D), BF),
        V((2, TOK, HALF_D + 128), F32), V((TOK, HALF_D + 128), F32),
        V((2, 3, 4, 4, 4, PAIR, CARRY), BF),
        V((2, HID, HALF_D), BF), V((4, SLOTS, HALF_D), BF), V((4, CHUNK, 256), BF),
        V((4, 4, 4, PAIR, HID), F32), V((4, 4, 4, PAIR, HID), F32),
        V((4, SLOTS, CHUNK), BF), V((4 * SLOTS, 128), F32), V((1024, 128), F32),
        V((4, CHUNK, 256), BF), V((2, 4 * SLOTS, HALF_D), BF), V((4 * SLOTS, HALF), BF),
    ]
    scratch += [V((4, 4, 4, PAIR, w), BF) for w in WIDTHS]
    scratch += [V((2, 2, 4, PAIR, w), BF) for w in WIDTHS]
    scratch += [V((2, 4, 4, PAIR, w), BF) for w in WIDTHS]
    scratch += [V((3, 4, PAIR, w), BF) for w in WIDTHS]
    scratch += [V((3, PAIR, w), BF) for w in WIDTHS]
    scratch += [V((2, TOK, HALF_D), F32), V((TOK, HALF_D), F32)]
    scratch += [
        dma((8,)), dma((4,)), dma((8,)), dma((8,)), dma((3,)), dma((3,)), dma((4,)),
        dma((N_AG,)), dma((N_AG,)), dma((N_RS,)), dma((N_RS,)),
    ]
    both = pl.pallas_call(
        kernel,
        out_shape=jax.ShapeDtypeStruct((2, TOK, D), BF),
        in_specs=[vm, hbm, vm, vm, vm, hbm, hbm, hbm, hbm, hbm, hbm, vm, vm],
        out_specs=vm,
        scratch_shapes=scratch,
        compiler_params=pltpu.CompilerParams(
            collective_id=0, has_side_effects=True, vmem_limit_bytes=63 * 1024 * 1024
        ),
    )(
        attn_heads, out_weight, residual, norm_gain, shared_gate,
        shared_gate_proj.T, shared_up_proj.T, shared_down_proj, expert_gate, expert_up_weight,
        expert_down, expert_choice, gate_probs,
    )
    return both[0], both[1]


def solution(mesh):
    both = ("dp", "tensor")
    in_specs = (
        P("dp", "tensor"), P("tensor", None), P(both, None), P(), P(),
        P(None, both), P(None, both), P(both, None),
        P(both, None, None), P(both, None, None), P(both, None, None),
        P(both, None), P(both, None),
    )
    out_specs = (P(both, None), P(both, None))
    return jax.shard_map(
        on_device, mesh=mesh, in_specs=in_specs, out_specs=out_specs, check_vma=False
    )
```

```python
import jax
import jax.numpy as jnp
from jax import lax
from jax.experimental import pallas as pl
from jax.experimental.pallas import tpu as pltpu
from jax.sharding import PartitionSpec as P

MESH = pl.DeviceIdType.MESH
BF = jnp.bfloat16
F32 = jnp.float32
TOK = 8
PAIR = 16
D = 3584
HALF_D = D // 2
WIDTHS = (640, 640, 512)
OFFS = (0, 640, 1280)
CARRY = 640
ORDERS = ((2, 1, 0), (1, 0, 2), (0, 2, 1))
HID = 160
HALF = 640
EXPERTS = 64
CHUNK = 256
SLOTS = 64
N_AG = 3 * (3 + 3 + 6 + 4)
N_RS = 3 * (6 + 3 + 3)


def silu(v):
    return v / (1.0 + jnp.exp(-v))


def kernel(
    heads, out_w, residual, gain, sgate, sgp, sup, sdn, eg, eu, ed, choice, probs,
    both_out,
    wo, wsg, wsu, weg, weu, wed, rhs,
    part, sbuf, rz, nx, rx, g,
    wd, res, lhs_in, acc_g, acc_u, place, pslot, share_s, lhs, xe, he,
    s0, s1, s2,
    a0, a1, a2, b0, b1, b2, c0, c1, c2, d0, d1, d2,
    fin, rfin,
    w_sem, again_sem, sib_s, sib_r, zs_sem, zr_sem, x_sem, ags, agr, rss, rsr,
):
    dp = lax.axis_index("dp")
    z0 = lax.axis_index("tensor")
    core = lax.rem(dp, 2)
    other = 1 - core
    pos = (dp // 8, lax.rem(dp // 2, 4), z0)

    def device(y, x, c, z):
        return ((y * 4 + x) * 2 + c, z)

    def near(axis, k):
        return lax.rem(pos[axis] + k, 4)

    def peer(axis, k):
        at = list(pos)
        at[axis] = near(axis, k)
        return device(at[0], at[1], core, at[2])

    sibling = device(pos[0], pos[1], other, pos[2])

    wo_load = pltpu.make_async_copy(out_w, wo, w_sem.at[0])
    loads = [
        pltpu.make_async_copy(sgp, wsg, w_sem.at[1]),
        pltpu.make_async_copy(sup, wsu, w_sem.at[2]),
        pltpu.make_async_copy(eg.at[0], weg, w_sem.at[3]),
        pltpu.make_async_copy(eu.at[0], weu, w_sem.at[4]),
        pltpu.make_async_copy(ed.at[0], wed, w_sem.at[5]),
    ]
    for h in range(2):
        cols = pl.ds(h * HALF_D, HALF_D)
        loads.append(pltpu.make_async_copy(sdn.at[:, cols], wd.at[h], w_sem.at[6 + h]))
    wo_load.start()
    for load in loads[0:4]:
        load.start()

    barrier = pltpu.get_barrier_semaphore()
    for k in (2, 1, 3):
        for axis in (2, 1, 0):
            pl.semaphore_signal(barrier, inc=1, device_id=peer(axis, k), device_id_type=MESH)
    pl.semaphore_signal(barrier, inc=1, device_id=sibling, device_id_type=MESH)

    def project(j, carry):
        at = pl.multiple_of(j * 256, 256)
        cols = pl.ds(at, 256)
        left = jnp.dot(heads[...], wo[:, cols], preferred_element_type=F32)
        right = jnp.dot(
            heads[...], wo[:, pl.ds(at + HALF_D, 256)], preferred_element_type=F32
        )
        part[0, :, :, cols] = left.reshape(4, TOK, 256)
        part[1, :, :, cols] = right.reshape(4, TOK, 256)
        for q in range(4):
            rows = slice(q * TOK, (q + 1) * TOK)
            sbuf[q, :, cols] = jnp.concatenate([left[rows], right[rows]], axis=0).astype(BF)
        return carry

    wo_load.wait()
    lax.fori_loop(0, 7, project, 0, unroll=True)

    pl.semaphore_wait(barrier, 10)

    zc = []
    for k in (2, 1, 3):
        c = pltpu.make_async_remote_copy(
            src_ref=sbuf.at[near(2, k)], dst_ref=rz.at[k - 1],
            send_sem=zs_sem.at[k - 1], recv_sem=zr_sem.at[k - 1],
            device_id=peer(2, k), device_id_type=MESH,
        )
        c.start()
        zc.append(c)

    rhs[:, :, HID + SLOTS : 256, :] = jnp.zeros((2, 4, 256 - HID - SLOTS, HALF_D), BF)

    lane = lax.broadcasted_iota(jnp.int32, (TOK, 128), 1)
    facts = jnp.zeros((TOK, 128), F32)
    chosen = choice[...].astype(F32)
    weight = probs[...]
    high = weight.astype(BF).astype(F32)
    low = weight - high
    for k in range(8):
        facts = jnp.where(lane == k, chosen[:, k : k + 1], facts)
        facts = jnp.where(lane == 8 + k, high[:, k : k + 1], facts)
        facts = jnp.where(lane == 16 + k, low[:, k : k + 1], facts)

    for c in zc:
        c.wait_recv()

    square = jnp.zeros((TOK, 1), F32)
    logit = jnp.zeros((TOK, 1), F32)
    mids = []
    for h in range(2):
        cols = slice(h * HALF_D, (h + 1) * HALF_D)
        total = part[h, z0]
        for k in range(3):
            total = total + rz[k].astype(F32)[h * TOK : (h + 1) * TOK]
        mid = (residual[:, cols].astype(F32) + total).astype(BF)
        both_out[0, :, cols] = mid
        midf = mid.astype(F32)
        mids.append(midf)
        square = square + jnp.sum(midf * midf, axis=1, keepdims=True)
        toward = gain[cols].astype(F32).reshape(1, HALF_D) * sgate[cols].astype(F32).reshape(1, HALF_D)
        logit = logit + jnp.sum(midf * toward, axis=1, keepdims=True)
    scale = lax.rsqrt(square * (1.0 / D) + 1e-06)
    for h in range(2):
        cols = slice(h * HALF_D, (h + 1) * HALF_D)
        normed = (mids[h] * scale * gain[cols].astype(F32).reshape(1, HALF_D)).astype(BF).astype(F32)
        nx[h, :, 0:HALF_D] = normed
    share = 1.0 / (1.0 + jnp.exp(-logit * scale))

    share_high = share.astype(BF).astype(F32)
    facts = jnp.where(lane == 24, share_high, facts)
    facts = jnp.where(lane == 25, share - share_high, facts)
    for h in range(2):
        nx[h, :, HALF_D : HALF_D + 128] = facts

    swap = pltpu.make_async_remote_copy(
        src_ref=nx.at[other], dst_ref=rx, send_sem=x_sem.at[0], recv_sem=x_sem.at[1],
        device_id=sibling, device_id_type=MESH,
    )
    swap.start()
    swap.wait_recv()
    mine = nx[core]
    theirs = rx[...]
    first = core == 0
    block = jnp.concatenate(
        [jnp.where(first, mine, theirs), jnp.where(first, theirs, mine)], axis=0
    ).astype(BF)
    for o in range(3):
        g[core, o, pos[0], pos[1], pos[2]] = block[:, o * CARRY : (o + 1) * CARRY]

    again = []
    for y in range(4):
        again.append(
            pltpu.make_async_copy(wd.at[core], rhs.at[0, y, pl.ds(0, HID)], again_sem.at[y])
        )

    def to_sibling(i, src, dst):
        return pltpu.make_async_remote_copy(
            src_ref=src, dst_ref=dst, send_sem=sib_s.at[i], recv_sem=sib_r.at[i],
            device_id=sibling, device_id_type=MESH,
        )

    across = [to_sibling(y, wd.at[other], rhs.at[1, y, pl.ds(0, HID)]) for y in range(4)]

    pending = []
    count = [0]

    def gsend(o, at, dev):
        i = count[0]
        count[0] += 1
        ref = g.at[(core, o) + tuple(at)]
        c = pltpu.make_async_remote_copy(
            src_ref=ref, dst_ref=ref, send_sem=ags.at[i], recv_sem=agr.at[i],
            device_id=dev, device_id_type=MESH,
        )
        c.start()
        pending.append(c)
        return c

    def where_(o, first_, second, third):
        at = [None, None, None]
        for axis, v in zip(ORDERS[o], (first_, second, third)):
            at[axis] = v
        return at

    ALL, A, B = pl.ds(0, 4), pl.ds(0, 2), pl.ds(2, 2)
    own = [[pos[axis] for axis in ORDERS[o]] for o in range(3)]

    got = [[], [], []]
    for k in (2, 1, 3):
        for o in range(3):
            got[o].append(gsend(o, pos, peer(ORDERS[o][0], k)))
    for load in loads[4:]:
        load.start()
    acc_g[...] = jnp.zeros((4, 4, 4, PAIR, HID), F32)
    acc_u[...] = jnp.zeros((4, 4, 4, PAIR, HID), F32)
    for load in loads[0:4]:
        load.wait()

    def absorb(h, o, k):
        at = tuple(where_(o, ALL, ALL, near(ORDERS[o][2], k)))
        x = g[(h, o) + at].reshape(CHUNK, CARRY)[:, : WIDTHS[o]]
        cols = pl.ds(pl.multiple_of(h * HALF_D + OFFS[o], 128), WIDTHS[o])
        turn = (((1,), (1,)), ((), ()))
        for acc, w in ((acc_g, wsg), (acc_u, wsu)):
            r = lax.dot_general(x, w[:, cols], turn, preferred_element_type=F32)
            acc[at] = acc[at] + r.reshape(4, 4, PAIR, HID)

    hop = []
    for o in range(3):
        for c in got[o]:
            c.wait_recv()
        mine_at = where_(o, ALL, own[o][1], own[o][2])
        hop.append([gsend(o, mine_at, peer(ORDERS[o][1], k)) for k in (2, 1, 3)])
    for load in loads[4:]:
        load.wait()
    for copy in again + across:
        copy.start()
    stage = []
    sib = [[], [], []]
    for o in range(3):
        for c in hop[o]:
            c.wait_recv()
        ax = ORDERS[o][2]
        at_a = where_(o, A, ALL, own[o][2])
        at_b = where_(o, B, ALL, own[o][2])
        ra = gsend(o, at_a, peer(ax, 1))
        lb = gsend(o, at_b, peer(ax, 3))
        rb = gsend(o, at_b, peer(ax, 1))
        la = gsend(o, at_a, peer(ax, 3))
        stage.append((ra, lb, rb, la))
        sib[o].append(gsend(o, where_(o, ALL, ALL, own[o][2]), sibling))
    for o in range(3):
        absorb(core, o, 0)
    for o in range(3):
        sib[o][0].wait_recv()
        absorb(other, o, 0)
    hop = [[], [], []]
    for event in range(4):
        for o in range(3):
            ax = ORDERS[o][2]
            half = (A, B, B, A)[event]
            came = near(ax, (3, 1, 3, 1)[event])
            at = where_(o, half, ALL, came)
            stage[o][event].wait_recv()
            if event < 2:
                hop[o].append(gsend(o, at, peer(ax, (1, 3)[event])))
            if event >= 2:
                sib[o].append(gsend(o, where_(o, ALL, ALL, came), sibling))
    for o in range(3):
        absorb(core, o, 3)
        absorb(core, o, 1)
    for o in range(3):
        sib[o][1].wait_recv()
        absorb(other, o, 3)
        sib[o][2].wait_recv()
        absorb(other, o, 1)
    for o in range(3):
        for c in hop[o]:
            c.wait_recv()
        sib[o].append(gsend(o, where_(o, ALL, ALL, near(ORDERS[o][2], 2)), sibling))

    expert = lax.rem(dp * 4 + z0, EXPERTS).astype(F32)
    told = g[core, 2, :, :, :, :, 512:640].reshape(1024, 128).astype(F32)
    share_s[...] = jnp.broadcast_to(told[:, 24:25] + told[:, 25:26], (1024, 128))
    turned = told.T
    hit8 = turned[0:8] == expert
    p_row = jnp.sum(jnp.where(hit8, turned[8:16] + turned[16:24], 0.0), axis=0, keepdims=True)
    hit = jnp.sum(jnp.where(hit8, 1.0, 0.0), axis=0, keepdims=True)
    hit = jnp.broadcast_to(hit, (8, 1024))
    token = lax.broadcasted_iota(jnp.int32, (8, 1024), 1)
    rank = jnp.zeros((8, 1024), F32)
    for k in range(1, 8):
        rank = rank + jnp.where(lax.rem(token, 8) >= k, pltpu.roll(hit, k, axis=1), 0.0)
    row = (lax.rem(token // 8, 32) * 2).astype(F32) + rank
    row = jnp.where(hit > 0.5, row, -1000.0)
    row1 = row[0:1]
    column = jnp.broadcast_to(row1, (128, 1024)).T
    lane1 = lax.broadcasted_iota(jnp.int32, (1024, 128), 1).astype(F32)
    lhs[:, :, 0:128] = jnp.zeros((4, CHUNK, 128), BF)
    lhs[:, :, 128:256] = (
        jnp.where(lane1 - (HID - 128.0) == column, 1.0, 0.0).astype(BF).reshape(4, CHUNK, 128)
    )
    slot_id = lax.broadcasted_iota(jnp.int32, (SLOTS, CHUNK), 0).astype(F32)
    for y in range(4):
        cols = slice(y * CHUNK, (y + 1) * CHUNK)
        chosen_y = jnp.where(slot_id == row1[:, cols], 1.0, 0.0)
        place[y] = chosen_y.astype(BF)
        pslot[pl.ds(y * SLOTS, SLOTS)] = jnp.broadcast_to(
            jnp.sum(chosen_y * p_row[:, cols], axis=1, keepdims=True), (SLOTS, 128)
        )

    def pick(h):
        for y in range(4):
            for o in range(3):
                x = g[h, o, y].reshape(CHUNK, CARRY)[:, : WIDTHS[o]]
                r = jnp.dot(place[y], x, preferred_element_type=F32)
                xe[h, y * SLOTS : (y + 1) * SLOTS, OFFS[o] : OFFS[o] + WIDTHS[o]] = r.astype(BF)

    for o in range(3):
        absorb(core, o, 2)
    pick(core)
    for o in range(3):
        sib[o][3].wait_recv()
        absorb(other, o, 2)
    pick(other)
    for y in range(4):
        share_y = share_s[y * CHUNK : (y + 1) * CHUNK]
        hs = silu(acc_g[y].reshape(CHUNK, HID)) * acc_u[y].reshape(CHUNK, HID)
        lhs[y, :, 0:128] = (hs[:, 0:128] * share_y).astype(BF)
        lhs[y, :, 128:HID] = (hs[:, 128:HID] * share_y[:, 0 : HID - 128]).astype(BF)

    lhs_over = to_sibling(4, lhs, lhs_in)
    lhs_over.start()

    def expert_hidden(i, carry):
        cols = pl.ds(pl.multiple_of(i * 128, 128), 128)
        w = jnp.concatenate([weg[:, cols], weu[:, cols]], axis=1)
        rows = jnp.concatenate([xe[0], xe[1]], axis=1)
        r = jnp.dot(rows, w, preferred_element_type=F32)
        he[:, cols] = (silu(r[:, 0:128]) * r[:, 128:256]).astype(BF)
        return carry

    lax.fori_loop(0, HALF // 128, expert_hidden, 0, unroll=True)

    def expert_down(h, at, w):
        cols = pl.ds(pl.multiple_of(h * HALF_D + at, 128), w)
        r = jnp.dot(he[...], wed[:, cols], preferred_element_type=F32)
        return (r * jnp.concatenate([pslot[...]] * (w // 128), axis=1)).astype(BF)

    res_over = []
    for o in range(3):
        cols = slice(OFFS[o], OFFS[o] + WIDTHS[o])
        down = expert_down(other, OFFS[o], WIDTHS[o])
        res[:, :, cols] = down.reshape(4, SLOTS, WIDTHS[o])
        cols = pl.ds(OFFS[o], WIDTHS[o])
        over = to_sibling(5 + o, res.at[:, :, cols], rhs.at[1, :, pl.ds(HID, SLOTS), cols])
        over.start()
        res_over.append(over)
    for o in range(3):
        cols = slice(OFFS[o], OFFS[o] + WIDTHS[o])
        down = expert_down(core, OFFS[o], WIDTHS[o])
        rhs[0, :, HID : HID + SLOTS, cols] = down.reshape(4, SLOTS, WIDTHS[o])
    for copy in again:
        copy.wait()
    for c in across + [lhs_over]:
        c.wait_recv()

    s = (s0, s1, s2)
    n_gather = len(pending)
    half_in = (a0, a1, a2)
    full_in = (b0, b1, b2)
    last_in = (c0, c1, c2)
    one_in = (d0, d1, d2)
    count[0] = 0

    def rsend(src, dst, dev):
        i = count[0]
        count[0] += 1
        c = pltpu.make_async_remote_copy(
            src_ref=src, dst_ref=dst, send_sem=rss.at[i], recv_sem=rsr.at[i],
            device_id=dev, device_id_type=MESH,
        )
        c.start()
        pending.append(c)
        return c

    def combine(o):
        cols = slice(OFFS[o], OFFS[o] + WIDTHS[o])
        for y in range(4):
            r = jnp.dot(lhs[y], rhs[0, y, :, cols], preferred_element_type=F32)
            r = r + jnp.dot(lhs_in[y], rhs[1, y, :, cols], preferred_element_type=F32)
            s[o][y] = r.astype(BF).reshape(4, 4, PAIR, WIDTHS[o])

    def at1(o, c, half):
        rest = [half, ALL]
        return tuple(c if axis == ORDERS[o][2] else rest.pop(0) for axis in range(3))

    def add1(o, c, lo, hi, terms):
        def step(i, carry):
            at = at1(o, c, i)
            total = s[o][at].astype(F32)
            for term, base in terms:
                total = total + term[i - base].astype(F32)
            s[o][at] = total.astype(BF)
            return carry

        lax.fori_loop(lo, hi, step, 0)

    stage = [[], [], []]
    for o in range(3):
        res_over[o].wait_recv()
        combine(o)
        ax = ORDERS[o][2]
        far = near(ax, 2)
        stage[o] += [
            rsend(s[o].at[at1(o, far, A)], half_in[o].at[0], peer(ax, 1)),
            rsend(s[o].at[at1(o, far, B)], half_in[o].at[1], peer(ax, 3)),
            rsend(s[o].at[at1(o, near(ax, 1), B)], full_in[o].at[0, B], peer(ax, 1)),
            rsend(s[o].at[at1(o, near(ax, 3), A)], full_in[o].at[1, A], peer(ax, 3)),
        ]
    for c in zc + [swap] + across + [lhs_over] + res_over + pending[:n_gather]:
        c.wait_send()
    for o in range(3):
        ax = ORDERS[o][2]
        c = near(ax, 1)
        stage[o][0].wait_recv()
        add1(o, c, 0, 2, [(half_in[o].at[0], 0)])
        stage[o].append(rsend(s[o].at[at1(o, c, A)], full_in[o].at[0, A], peer(ax, 1)))
        c = near(ax, 3)
        stage[o][1].wait_recv()
        add1(o, c, 2, 4, [(half_in[o].at[1], 2)])
        stage[o].append(rsend(s[o].at[at1(o, c, B)], full_in[o].at[1, B], peer(ax, 3)))

    def at2(o, c):
        return tuple(where_(o, ALL, c, own[o][2]))

    def line_sum(o, c):
        rest = [axis for axis in range(3) if axis != ORDERS[o][2]]
        at = (c,) if rest[0] == ORDERS[o][1] else (ALL, c)
        total = s[o][at2(o, c)].astype(F32)
        for side in range(2):
            total = total + full_in[o][(side,) + at].astype(F32)
        return total

    stage2 = []
    for o in range(3):
        for c in stage[o][2:]:
            c.wait_recv()
        ax = ORDERS[o][1]
        sent = []
        for k in (2, 1, 3):
            at = at2(o, near(ax, k))
            s[o][at] = line_sum(o, near(ax, k)).astype(BF)
            sent.append(rsend(s[o].at[at], last_in[o].at[k - 1], peer(ax, k)))
        stage2.append(sent)

    for c in pending[n_gather : n_gather + 18]:
        c.wait_send()
    stage3 = []
    for o in range(3):
        for c in stage2[o]:
            c.wait_recv()
        at = at2(o, own[o][1])
        total = line_sum(o, own[o][1])
        for k in range(3):
            total = total + last_in[o][k].astype(F32)
        s[o][at] = total.astype(BF)
        ax = ORDERS[o][0]
        stage3.append(
            [
                rsend(
                    s[o].at[tuple(where_(o, near(ax, k), own[o][1], own[o][2]))],
                    one_in[o].at[k - 1],
                    peer(ax, k),
                )
                for k in (2, 1, 3)
            ]
        )
    for o in range(3):
        total = s[o][pos].astype(F32)
        for c in stage3[o]:
            c.wait_recv()
        for k in range(3):
            total = total + one_in[o][k].astype(F32)
        cols = pl.ds(OFFS[o], WIDTHS[o])
        fin[0, :, cols] = total[0:TOK]
        fin[1, :, cols] = total[TOK:PAIR]

    swap_back = pltpu.make_async_remote_copy(
        src_ref=fin.at[other], dst_ref=rfin, send_sem=x_sem.at[2], recv_sem=x_sem.at[3],
        device_id=sibling, device_id_type=MESH,
    )
    swap_back.start()
    swap_back.wait_recv()
    mine = fin[core]
    theirs = rfin[...]
    both_out[1, :, 0:HALF_D] = jnp.where(first, mine, theirs).astype(BF)
    both_out[1, :, HALF_D:D] = jnp.where(first, theirs, mine).astype(BF)

    swap_back.wait_send()
    for c in pending[n_gather + 18 :]:
        c.wait_send()


def on_device(
    attn_heads, out_weight, residual, norm_gain, shared_gate, shared_gate_proj, shared_up_proj,
    shared_down_proj, expert_gate, expert_up_weight, expert_down, expert_choice, gate_probs,
):
    vm = pl.BlockSpec(memory_space=pltpu.VMEM)
    hbm = pl.BlockSpec(memory_space=pl.ANY)
    V = pltpu.VMEM
    dma = pltpu.SemaphoreType.DMA
    scratch = [
        V((896, D), BF), V((HID, D), BF), V((HID, D), BF),
        V((D, HALF), BF), V((D, HALF), BF), V((HALF, D), BF), V((2, 4, 256, HALF_D), BF),
        V((2, 4, TOK, HALF_D), F32), V((4, PAIR, HALF_D), BF), V((3, PAIR, HALF_D), BF),
        V((2, TOK, HALF_D + 128), F32), V((TOK, HALF_D + 128), F32),
        V((2, 3, 4, 4, 4, PAIR, CARRY), BF),
        V((2, HID, HALF_D), BF), V((4, SLOTS, HALF_D), BF), V((4, CHUNK, 256), BF),
        V((4, 4, 4, PAIR, HID), F32), V((4, 4, 4, PAIR, HID), F32),
        V((4, SLOTS, CHUNK), BF), V((4 * SLOTS, 128), F32), V((1024, 128), F32),
        V((4, CHUNK, 256), BF), V((2, 4 * SLOTS, HALF_D), BF), V((4 * SLOTS, HALF), BF),
    ]
    scratch += [V((4, 4, 4, PAIR, w), BF) for w in WIDTHS]
    scratch += [V((2, 2, 4, PAIR, w), BF) for w in WIDTHS]
    scratch += [V((2, 4, 4, PAIR, w), BF) for w in WIDTHS]
    scratch += [V((3, 4, PAIR, w), BF) for w in WIDTHS]
    scratch += [V((3, PAIR, w), BF) for w in WIDTHS]
    scratch += [V((2, TOK, HALF_D), F32), V((TOK, HALF_D), F32)]
    scratch += [
        dma((8,)), dma((4,)), dma((8,)), dma((8,)), dma((3,)), dma((3,)), dma((4,)),
        dma((N_AG,)), dma((N_AG,)), dma((N_RS,)), dma((N_RS,)),
    ]
    both = pl.pallas_call(
        kernel,
        out_shape=jax.ShapeDtypeStruct((2, TOK, D), BF),
        in_specs=[vm, hbm, vm, vm, vm, hbm, hbm, hbm, hbm, hbm, hbm, vm, vm],
        out_specs=vm,
        scratch_shapes=scratch,
        compiler_params=pltpu.CompilerParams(
            collective_id=0, has_side_effects=True, vmem_limit_bytes=63 * 1024 * 1024
        ),
    )(
        attn_heads, out_weight, residual, norm_gain, shared_gate,
        shared_gate_proj.T, shared_up_proj.T, shared_down_proj, expert_gate, expert_up_weight,
        expert_down, expert_choice, gate_probs,
    )
    return both[0], both[1]


def solution(mesh):
    both = ("dp", "tensor")
    in_specs = (
        P("dp", "tensor"), P("tensor", None), P(both, None), P(), P(),
        P(None, both), P(None, both), P(both, None),
        P(both, None, None), P(both, None, None), P(both, None, None),
        P(both, None), P(both, None),
    )
    out_specs = (P(both, None), P(both, None))
    return jax.shard_map(
        on_device, mesh=mesh, in_specs=in_specs, out_specs=out_specs, check_vma=False
    )
```
